256 devices in a mesh: group: 8 (over z), shard: 32 (over x, y, core).
Axes of the slice: x: 4, y: 4, z: 8, core: 2. Of those that a mesh axis runs over, the one named last changes fastest.
Arguments:
- gradient: float32 [37748736], P(('group', 'shard')), may hold values from -3000 to 3000
- momentum: float32 [37748736], P(('group', 'shard')), may hold values from -6 to 6
- master_weights: float32 [37748736], P(('group', 'shard')), may hold values from -0.3125 to 0.3125
- slot_table: int32 [24], replicated, may hold values from 0 to 23, as said below
Outputs:
- new_momentum: float32 [37748736], P(('group', 'shard'))
- update: float32 [37748736], P(('group', 'shard'))
- new_master: float32 [37748736], P(('group', 'shard'))
- weights: bfloat16 [37748736], P('group')
The draws below stay inside these ranges and needn't reach their ends.
Inputs may be any that keep to these rules, and one draw needn't show every extreme that they name: `slot_table`: each of 0 to 23 appears exactly once.
All inputs are finite; a program needn't handle non-finite values.
Results may differ from the reference program's by a relative error of at most 0.0066.
Values may be sent and summed in bfloat16 or wider, within the bound.
No kernel may reach another device: no remote copies, remote signals or barrier semaphores. Data moves between devices by JAX's collectives and lax.ppermute only.
A program may use at most 64 MiB of HBM per device.

```python
import math
import jax
import jax.numpy as jnp
from jax import lax

D = 2048
FF = 768
NS_ITERS = 2
MAT = 24
TOTAL = 37748736


def slot_order(key):
    return jax.random.permutation(key, MAT).astype(jnp.int32)


def draw_slot_table(key, part):
    return slot_order(key)


def draw_gradient(key, part):
    order = slot_order(key)
    key = jax.random.fold_in(key, 7)
    keys = jax.random.split(key, 3)
    matrix_len = D * FF
    indices = jnp.arange(MAT, dtype=jnp.int32)
    kinds = jnp.sum(jnp.where(order[:, None] == indices[None, :], (indices % 3)[:, None], 0), axis=0)
    flat = jnp.arange(TOTAL, dtype=jnp.int32)
    slot_index = flat // matrix_len
    inner = flat % matrix_len
    down = kinds[slot_index] == 2
    row_index = jnp.where(down, inner // D, inner // FF)
    col_index = jnp.where(down, inner % D, inner % FF)
    upper = math.log(10.0)
    row_scale = jnp.exp(jax.random.uniform(keys[0], (MAT, D), jnp.float32, 0.0, upper))
    col_scale = jnp.exp(jax.random.uniform(keys[1], (MAT, D), jnp.float32, 0.0, upper))
    ramp = jnp.exp(math.log(3.0) * flat.astype(jnp.float32) / TOTAL)
    noise = jnp.clip(jax.random.normal(keys[2], (TOTAL,), jnp.float32), -4.0, 4.0)
    return noise * row_scale[slot_index, row_index] * col_scale[slot_index, col_index] * ramp


def block_levels(key, extent, cuts, least, high):
    def one(dim, shards_of):
        draws = jax.random.uniform(jax.random.fold_in(jax.random.fold_in(key, 6), dim), (shards_of,), jnp.float32, least / len(cuts), high / len(cuts))
        return jnp.repeat(jnp.exp(draws), extent[dim] // shards_of).reshape((-1,) + (1,) * (len(extent) - dim - 1))

    factor_of = one(*cuts[0])
    for cut in cuts[1:]:
        factor_of = factor_of * one(*cut)
    return factor_of


def normal_values(rng, extent, deviation, most, shards=(), kind=jnp.bfloat16):
    drawn = deviation * jax.random.normal(rng, extent, jnp.float32)
    if shards:
        drawn = drawn * block_levels(rng, extent, shards, -0.22, 0.18)
    return jnp.clip(drawn, -most, most).astype(kind)


def setup_inputs(seed: int = 0) -> dict:
    key_of = jax.random.split(jax.random.key(seed), 5)
    return {
        "gradient": draw_gradient(jax.random.fold_in(key_of[4], 71), 0),
        "momentum": normal_values(key_of[1], (TOTAL,), 1.0, 6.0, ((0, 256),), jnp.float32),
        "master_weights": normal_values(key_of[2], (TOTAL,), 0.02, 0.3125, ((0, 256),), jnp.float32),
        "slot_table": draw_slot_table(jax.random.fold_in(key_of[4], 71), 0),
    }


coef_first = 3.4445
coef_second = -4.775
coef_third = 2.0315
beta_momentum = 0.95
learn_rate = 0.02
weight_decay = 0.1

def newton_schulz(flat, kind):
    tall = flat.reshape(D, FF).T
    wide = flat.reshape(FF, D)
    matrix = jnp.where(kind == 2, wide, tall)
    values = matrix.astype(jnp.float32)
    magnitude = jnp.sqrt(jnp.sum(values * values))
    state = (values / (magnitude + 1e-07)).astype(jnp.bfloat16)
    for counter in range(NS_ITERS):
        gram = jnp.dot(state, state.T, preferred_element_type=jnp.float32).astype(jnp.bfloat16)
        square = jnp.dot(gram, gram, preferred_element_type=jnp.float32)
        poly = (coef_second * gram.astype(jnp.float32) + coef_third * square).astype(jnp.bfloat16)
        state = (coef_first * state.astype(jnp.float32) + jnp.dot(poly, state, preferred_element_type=jnp.float32)).astype(jnp.bfloat16)
    return jnp.where(kind == 2, state.reshape(-1), state.T.reshape(-1))

def reference(gradient, momentum, master_weights, slot_table):
    total_sq = jnp.sum(gradient * gradient)
    clip_factor = jnp.minimum(1.0, 0.5 * math.sqrt(TOTAL) / jnp.sqrt(total_sq + 1e-06))
    clipped = clip_factor * gradient
    new_momentum = beta_momentum * momentum + clipped
    looked = (clipped + beta_momentum * new_momentum).astype(jnp.bfloat16)
    indices = jnp.arange(MAT, dtype=jnp.int32)
    kinds = lax.optimization_barrier(jnp.sum(jnp.where(slot_table[:, None] == indices[None, :], (indices % 3)[:, None], 0), axis=0)).astype(jnp.int32)
    blocks = looked.reshape(MAT, D * FF)
    solved = lax.map(lambda pair: newton_schulz(pair[0], pair[1]), (blocks, kinds))
    update = math.sqrt(D) * solved.reshape(-1).astype(jnp.float32)
    new_master = master_weights * (1.0 - learn_rate * weight_decay) - learn_rate * 0.2 * update
    weights = new_master.astype(jnp.bfloat16)
    return (new_momentum, update, new_master, weights)
```

```python
import math

import jax
import jax.numpy as jnp
from jax import lax
from jax.experimental import pallas as pl
from jax.experimental.pallas import tpu as pltpu
from jax.sharding import PartitionSpec as P

D = 2048
FF = 768
MATS = 3
UNITS = 32
SHARD_TILES = 72
SHARD_ROWS = 1152
MAT_ROWS = 12288
MAT_TILES = 768
WIDE = 256

coef_first = 3.4445
coef_second = -4.775
coef_third = 2.0315
beta_momentum = 0.95
learn_rate = 0.02
weight_decay = 0.1

f32 = jnp.float32
bf16 = jnp.bfloat16
MIB = 2**20

VM = pl.BlockSpec(memory_space=pltpu.VMEM)
SM = pl.BlockSpec(memory_space=pltpu.SMEM)
ANY = pl.BlockSpec(memory_space=pl.ANY)


def shard_of(x, y, c):
    return (x % 4) * 8 + (y % 4) * 2 + c


def first_route(step):
    route = []
    for x in range(4):
        for y in range(4):
            route.append((shard_of(x, y, 0), shard_of(x, y + step, 0)))
            route.append((shard_of(x, y, 1), shard_of(x + step, y, 1)))
    return route


def second_route(step):
    route = []
    for x in range(4):
        for y in range(4):
            route.append((shard_of(x, y, 0), shard_of(x + step, y, 0)))
            route.append((shard_of(x, y, 1), shard_of(x, y + step, 1)))
    return route


def swap_route():
    return [(s, s ^ 1) for s in range(32)]


def kind_of(info, matrix):
    kind = jnp.int32(0)
    for m in range(24):
        kind = jnp.where(info[m] == matrix, jnp.int32(m % 3), kind)
    return kind


def look_kernel(info, sums, g_ref, m_ref, nm_ref, look_ref, scratch):
    total = jnp.sum(sums[...], axis=0, keepdims=True)[:, :1]
    clip = jnp.minimum(1.0, 0.5 * math.sqrt(24 * D * FF) / jnp.sqrt(total + 1e-06))
    clipped = clip * g_ref[...]
    new_momentum = beta_momentum * m_ref[...] + clipped
    nm_ref[...] = new_momentum
    scratch[...] = clipped + beta_momentum * new_momentum
    group, shard = info[24], info[25]
    for t in range(3):
        kind = kind_of(info, 3 * group + (3 * shard + t) // UNITS)
        row = 384 * t

        @pl.when(kind != 2)
        def _():
            for a in range(4):
                for j in range(6):
                    tile = scratch[pl.ds(row + 96 * a + j, 16, stride=6), :]
                    look_ref[24 * t + 6 * a + j] = tile.astype(bf16)

        @pl.when(kind == 2)
        def _():
            for j in range(16):
                tile = scratch[pl.ds(row + j, 16, stride=16), :]
                look_ref[24 * t + j] = tile.astype(bf16)
            for q in range(8):
                low = scratch[pl.ds(row + 256 + q, 8, stride=16), :]
                high = scratch[pl.ds(row + 264 + q, 8, stride=16), :]
                look_ref[24 * t + 16 + q] = jnp.concatenate([low, high], 0).astype(bf16)


def tiles(x, first, count, stride):
    return jnp.concatenate([x[first + stride * i] for i in range(count)], 0)


def mm(a, b):
    return jnp.dot(a, b, preferred_element_type=f32)


def mm_t(a, b):
    return lax.dot_general(a, b, (((1,), (1,)), ((), ())), preferred_element_type=f32)


def orthogonalize(kind, base, x, wide, flat, a0, b0, wb, b1, total):
    @pl.when(kind == 2)
    def _():
        def pair(i, carry):
            t = base + 48 * i
            for h in range(2):
                rows = pl.ds(pl.multiple_of(32 * i + 16 * h, 16), 16)
                for j in range(16):
                    wide[rows, 128 * j : 128 * j + 128] = x[t + 24 * h + j]
            rows = pl.ds(pl.multiple_of(512 + 16 * i, 16), 16)
            for q in range(8):
                one = x[t + 16 + q].astype(f32)
                two = x[t + 40 + q].astype(f32)
                low = jnp.concatenate([one[:8], two[:8]], 0).astype(bf16)
                high = jnp.concatenate([one[8:], two[8:]], 0).astype(bf16)
                wide[rows, 128 * q : 128 * q + 128] = low
                wide[rows, 128 * (q + 8) : 128 * (q + 8) + 128] = high
            return carry

        lax.fori_loop(0, 16, pair, 0)

    @pl.when(kind != 2)
    def _():
        def chunk(i, carry):
            columns = pl.ds(pl.multiple_of(WIDE * i, WIDE), WIDE)
            for j in range(6):
                wide[128 * j : 128 * j + 128, columns] = tiles(x, base + 96 * i + j, 16, 6).T
            return carry

        lax.fori_loop(0, 8, chunk, 0)

    parts = [slice(WIDE * n, WIDE * n + WIDE) for n in range(3)]
    iota = lax.broadcasted_iota
    square_sum = jnp.zeros((1, 1), f32)
    for part in parts:
        total[:, part] = mm_t(wide[...], wide[part, :])
        block = total[part, part]
        same = iota(jnp.int32, (WIDE, WIDE), 0) == iota(jnp.int32, (WIDE, WIDE), 1)
        square_sum = square_sum + jnp.sum(jnp.where(same, block, 0.0), keepdims=True)
    inverse = 1.0 / (jnp.sqrt(square_sum) + 1e-07)
    for part in parts:
        a0[part, :] = (total[part, :] * inverse * inverse).astype(bf16)
    for part in parts:
        square = mm(a0[...], a0[:, part])
        b0[:, part] = (coef_second * a0[:, part].astype(f32) + coef_third * square).astype(bf16)
    for part in parts:
        step = coef_first * a0[:, part].astype(f32) + mm(a0[...], b0[:, part])
        total[:, part] = coef_first * step
        wb[:, part] = step.astype(bf16)
    a1 = a0
    for part in parts:
        a1[:, part] = (total[:, part] + mm(b0[...], wb[:, part])).astype(bf16)
    for part in parts:
        square = mm(a1[...], a1[:, part])
        b1[:, part] = (coef_second * a1[:, part].astype(f32) + coef_third * square).astype(bf16)
    scale = inverse * math.sqrt(D)
    rest = wb
    diagonal_row = []
    diagonal_column = jnp.zeros((FF, 1), f32)
    for n, part in enumerate(parts):
        both = b0[:, part].astype(f32) + b1[:, part].astype(f32)
        step = coef_first * both + mm(b1[...], b0[:, part])
        same = iota(jnp.int32, (FF, WIDE), 0) == iota(jnp.int32, (FF, WIDE), 1) + WIDE * n
        diagonal = jnp.where(same, step, 0.0)
        diagonal_row.append(jnp.sum(diagonal, axis=0, keepdims=True))
        diagonal_column = diagonal_column + jnp.sum(diagonal, axis=1, keepdims=True)
        rest[:, part] = jnp.where(same, 0.0, step).astype(bf16)
    diagonal_row = (jnp.concatenate(diagonal_row, 1) + coef_first * coef_first) * scale
    diagonal_column = (diagonal_column + coef_first * coef_first) * scale

    @pl.when(kind != 2)
    def _():
        def chunk(i, carry):
            block = jnp.concatenate([tiles(x, base + 96 * i + j, 16, 6) for j in range(6)], 1)
            moved = mm(block, rest[...]) * scale + block.astype(f32) * diagonal_row
            for j in range(6):
                rows = pl.ds(SHARD_ROWS + 1536 * i + j, WIDE, stride=6)
                flat[rows, :] = moved[:, 128 * j : 128 * j + 128]
            return carry

        lax.fori_loop(0, 8, chunk, 0)

    @pl.when(kind == 2)
    def _():
        def chunk(i, carry):
            block = wide[:, pl.ds(pl.multiple_of(WIDE * i, WIDE), WIDE)]
            moved = mm(rest[...], block) * scale + block.astype(f32) * diagonal_column
            for h in range(2):
                panel = moved[:, 128 * h : 128 * h + 128]
                start = SHARD_ROWS + 2 * i + h
                for u in range(UNITS):
                    rows = pl.ds(start + 384 * u, 16, stride=16)
                    flat[rows, :] = panel[16 * u : 16 * u + 16]
                    rows = pl.ds(start + 384 * u + 256, 8, stride=16)
                    flat[rows, :] = panel[512 + 8 * u : 512 + 8 * u + 8]
            return carry

        lax.fori_loop(0, 8, chunk, 0)


def matrix_kernel(last, n_sources, *refs):
    info, sources, refs = refs[0], refs[1 : 1 + n_sources], refs[1 + n_sources :]
    if last:
        master, _, weights, own = refs[:4]
        refs = refs[4:]
    else:
        master, weights, sent, own, other = refs[:5]
        refs = refs[5:]
    x, wide, flat, a0, b0, wb, b1, total, master_block, out_block, sems, more = refs
    group, shard = info[24], info[25]
    row, column, core = shard // 8, (shard // 2) % 4, shard % 2
    matrix = jnp.int32(2) if last else core
    first = (UNITS * matrix) // 3
    final = (UNITS * matrix + UNITS - 1) // 3
    matrix_rows = pl.ds(pl.multiple_of(MAT_ROWS * matrix, MAT_ROWS), MAT_ROWS)
    load_master = pltpu.make_async_copy(master.at[matrix_rows, :], master_block, more.at[0])
    load_master.start()

    loads = []
    for i, source in enumerate(sources):
        partner, (second, first_hops) = divmod(i, 8)[0], PLACES[i % 8]
        holder = core if partner == 0 else 1 - core
        for slot, hops in enumerate(first_hops):
            at_zero = shard_of(row - second + 4, column - hops + 4, 0)
            at_one = shard_of(row - hops + 4, column - second + 4, 1)
            place = jnp.where(holder == 0, at_zero, at_one)
            wanted = (place >= first) & (place <= final)
            target = SHARD_TILES * jnp.clip(place - first, 0, 11)
            copy = pltpu.make_async_copy(
                source.at[pl.ds(SHARD_TILES * slot, SHARD_TILES)],
                x.at[pl.ds(target, SHARD_TILES)],
                sems.at[2 * i + slot],
            )
            loads.append((wanted, copy))
    for wanted, copy in loads:
        pl.when(wanted)(copy.start)
    for wanted, copy in loads:
        pl.when(wanted)(copy.wait)

    kind = kind_of(info, 3 * group + matrix)
    base = MAT_TILES * matrix - SHARD_TILES * first
    orthogonalize(kind, base, x, wide, flat, a0, b0, wb, b1, total)

    def piece(who, out, sem):
        start = jnp.clip(SHARD_ROWS * (who + 1) - MAT_ROWS * matrix, 0, MAT_ROWS + SHARD_ROWS)
        start = pl.multiple_of(start, 128)
        return pltpu.make_async_copy(flat.at[pl.ds(start, SHARD_ROWS), :], out, sem)

    stores = [piece(shard, own, more.at[1])]
    if not last:
        stores.append(piece(shard + 1 - 2 * core, other, more.at[2]))
    for store in stores:
        store.start()
    load_master.wait()

    def weigh(i, carry):
        rows = pl.ds(pl.multiple_of(512 * i, 512), 512)
        update = flat[pl.ds(pl.multiple_of(SHARD_ROWS + 512 * i, 128), 512), :]
        kept = master_block[rows, :].astype(f32) * (1.0 - learn_rate * weight_decay)
        out_block[rows, :] = (kept - learn_rate * 0.2 * update).astype(bf16)
        return carry

    lax.fori_loop(0, MAT_ROWS // 512, weigh, 0)
    store = pltpu.make_async_copy(out_block, weights.at[matrix_rows, :], more.at[3])
    store.start()
    stores.append(store)
    if not last:
        store = pltpu.make_async_copy(out_block, sent, more.at[4])
        store.start()
        stores.append(store)
    for store in stores:
        store.wait()


PLACES = [
    (0, (0, 1)),
    (0, (2, 3)),
    (1, (0, 1)),
    (1, (2, 3)),
    (3, (0, 1)),
    (3, (2, 3)),
    (2, (0, 1)),
    (2, (2, 3)),
]

MATRIX_SCRATCH = [
    pltpu.VMEM((12 * SHARD_TILES, 16, 128), bf16),
    pltpu.VMEM((FF, D), bf16),
    pltpu.VMEM((MAT_ROWS + 2 * SHARD_ROWS, 128), f32),
    pltpu.VMEM((FF, FF), bf16),
    pltpu.VMEM((FF, FF), bf16),
    pltpu.VMEM((FF, FF), bf16),
    pltpu.VMEM((FF, FF), bf16),
    pltpu.VMEM((FF, FF), f32),
    pltpu.VMEM((MAT_ROWS, 128), bf16),
    pltpu.VMEM((MAT_ROWS, 128), bf16),
    pltpu.SemaphoreType.DMA((32,)),
    pltpu.SemaphoreType.DMA((5,)),
]


def finish_kernel(info, _, received, mine, theirs, third, master_ref, weights, update_ref, new_ref, sems):
    shard = info[25]
    core = shard % 2
    start = MAT_ROWS * (1 - core)
    quarter = MAT_ROWS // 4
    copies = []
    for i in range(4):
        rows = pl.ds(pl.multiple_of(start + quarter * i, quarter), quarter)
        copy = pltpu.make_async_copy(
            received.at[pl.ds(quarter * i, quarter), :], weights.at[rows, :], sems.at[i]
        )
        copy.start()
        copies.append(copy)
    for t in range(3):
        matrix = (3 * shard + t) // UNITS
        rows = slice(384 * t, 384 * t + 384)

        @pl.when(matrix == core)
        def _():
            update_ref[rows, :] = mine[rows, :]

        @pl.when(matrix == 1 - core)
        def _():
            update_ref[rows, :] = theirs[rows, :]

        @pl.when(matrix == 2)
        def _():
            update_ref[rows, :] = third[rows, :]

    kept = master_ref[...] * (1.0 - learn_rate * weight_decay)
    new_ref[...] = kept - learn_rate * 0.2 * update_ref[...]
    for copy in copies:
        copy.wait()


def params(mib):
    return pltpu.CompilerParams(vmem_limit_bytes=mib * MIB)


def on_device(gradient, momentum, master_weights, slot_table):
    place = jnp.stack([lax.axis_index("group"), lax.axis_index("shard")]).astype(jnp.int32)
    info = jnp.concatenate([slot_table, place])
    gathered = lax.all_gather(master_weights.astype(bf16), "shard", axis=0, tiled=True)
    gathered = gathered.reshape(MATS * MAT_ROWS, 128)

    own_sq = jnp.sum(gradient * gradient)
    sums = lax.all_to_all(jnp.full((32, 128), own_sq, f32), "shard", 0, 0)
    sums = jnp.broadcast_to(jnp.sum(sums, axis=0, keepdims=True), (8, 128))
    sums = lax.all_to_all(sums, "group", 0, 0)

    flat_shape = jax.ShapeDtypeStruct((SHARD_ROWS, 128), f32)
    new_momentum, look = pl.pallas_call(
        look_kernel,
        out_shape=(flat_shape, jax.ShapeDtypeStruct((SHARD_TILES, 16, 128), bf16)),
        in_specs=[SM, VM, VM, VM],
        out_specs=(VM, VM),
        scratch_shapes=[pltpu.VMEM((SHARD_ROWS, 128), f32)],
        compiler_params=params(8),
    )(info, sums, gradient.reshape(SHARD_ROWS, 128), momentum.reshape(SHARD_ROWS, 128))

    def send(block, route):
        return lax.ppermute(block, "shard", route)

    near = send(look, first_route(1))
    far = send(look, first_route(2))
    back = send(look, first_route(3))
    ahead = jnp.concatenate([look, near])
    behind = jnp.concatenate([far, back])
    sources = [ahead, behind]
    forward = [send(ahead, second_route(1)), send(behind, second_route(1))]
    backward = [send(ahead, second_route(3)), send(behind, second_route(3))]
    across = [send(forward[0], second_route(1)), send(backward[1], second_route(3))]
    sources = sources + forward + backward + across
    sources = sources + [send(block, swap_route()) for block in sources]

    weights_shape = jax.ShapeDtypeStruct((MATS * MAT_ROWS, 128), bf16)
    cost = pl.CostEstimate(flops=9_300_000_000, bytes_accessed=20_000_000, transcendentals=0)
    weights, sent, mine, other = pl.pallas_call(
        lambda *refs: matrix_kernel(False, 16, *refs),
        out_shape=(weights_shape, jax.ShapeDtypeStruct((MAT_ROWS, 128), bf16), flat_shape, flat_shape),
        in_specs=[SM] + [ANY] * 17,
        out_specs=(ANY, ANY, ANY, ANY),
        scratch_shapes=MATRIX_SCRATCH,
        compiler_params=params(60),
        cost_estimate=cost,
    )(info, *sources, gathered)
    received = send(sent, swap_route())
    theirs = send(other, swap_route())
    weights, third = pl.pallas_call(
        lambda *refs: matrix_kernel(True, 16, *refs),
        out_shape=(weights_shape, flat_shape),
        in_specs=[SM] + [ANY] * 18,
        out_specs=(ANY, ANY),
        scratch_shapes=MATRIX_SCRATCH,
        input_output_aliases={18: 0},
        compiler_params=params(60),
        cost_estimate=cost,
    )(info, *sources, gathered, weights)
    weights, update, new_master = pl.pallas_call(
        finish_kernel,
        out_shape=(weights_shape, flat_shape, flat_shape),
        in_specs=[SM, ANY, VM, VM, VM, VM, VM],
        out_specs=(ANY, VM, VM),
        scratch_shapes=[pltpu.SemaphoreType.DMA((4,))],
        input_output_aliases={1: 0},
        compiler_params=params(16),
    )(info, weights, received, mine, theirs, third, master_weights.reshape(SHARD_ROWS, 128))
    return (
        new_momentum.reshape(-1),
        update.reshape(-1),
        new_master.reshape(-1),
        weights.reshape(-1),
    )


def solution(mesh):
    in_specs = (P(("group", "shard")), P(("group", "shard")), P(("group", "shard")), P())
    out_specs = (P(("group", "shard")), P(("group", "shard")), P(("group", "shard")), P("group"))
    return jax.shard_map(
        on_device, mesh=mesh, in_specs=in_specs, out_specs=out_specs, check_vma=False
    )
```

```python
import math

import jax
import jax.numpy as jnp
from jax import lax
from jax.experimental import pallas as pl
from jax.experimental.pallas import tpu as pltpu
from jax.sharding import PartitionSpec as P

D = 2048
FF = 768
MATS = 3
UNITS = 32
SHARD_TILES = 72
SHARD_ROWS = 1152
MAT_ROWS = 12288
MAT_TILES = 768
WIDE = 256

coef_first = 3.4445
coef_second = -4.775
coef_third = 2.0315
beta_momentum = 0.95
learn_rate = 0.02
weight_decay = 0.1

f32 = jnp.float32
bf16 = jnp.bfloat16
MIB = 2**20

VM = pl.BlockSpec(memory_space=pltpu.VMEM)
SM = pl.BlockSpec(memory_space=pltpu.SMEM)
ANY = pl.BlockSpec(memory_space=pl.ANY)


def shard_of(x, y, c):
    return (x % 4) * 8 + (y % 4) * 2 + c


def first_route(step):
    route = []
    for x in range(4):
        for y in range(4):
            route.append((shard_of(x, y, 0), shard_of(x, y + step, 0)))
            route.append((shard_of(x, y, 1), shard_of(x + step, y, 1)))
    return route


def second_route(step):
    route = []
    for x in range(4):
        for y in range(4):
            route.append((shard_of(x, y, 0), shard_of(x + step, y, 0)))
            route.append((shard_of(x, y, 1), shard_of(x, y + step, 1)))
    return route


def swap_route():
    return [(s, s ^ 1) for s in range(32)]


def kind_of(info, matrix):
    kind = jnp.int32(0)
    for m in range(24):
        kind = jnp.where(info[m] == matrix, jnp.int32(m % 3), kind)
    return kind


def opening_kernel(g_ref, master_ref, sums_ref, narrow_ref):
    gradient = g_ref[...]
    rows = jnp.sum((gradient * gradient).reshape(SHARD_ROWS // 8, 8, 128), axis=0)
    total = jnp.sum(jnp.sum(rows, axis=0, keepdims=True), axis=1, keepdims=True)
    sums_ref[...] = jnp.broadcast_to(total, (32, 128))
    narrow_ref[...] = master_ref[...].astype(bf16)


def join_kernel(*refs):
    outs = refs[4:]
    length = refs[0].shape[0]
    per = 4 // len(outs)
    for i, ref in enumerate(refs[:4]):
        start = length * (i % per)
        outs[i // per][start : start + length] = ref[...]


def look_kernel(info, sums, g_ref, m_ref, nm_ref, look_ref, scratch):
    total = jnp.sum(sums[...], axis=0, keepdims=True)[:, :1]
    clip = jnp.minimum(1.0, 0.5 * math.sqrt(24 * D * FF) / jnp.sqrt(total + 1e-06))
    clipped = clip * g_ref[...]
    new_momentum = beta_momentum * m_ref[...] + clipped
    nm_ref[...] = new_momentum
    scratch[...] = clipped + beta_momentum * new_momentum
    group, shard = info[24], info[25]
    for t in range(3):
        kind = kind_of(info, 3 * group + (3 * shard + t) // UNITS)
        row = 384 * t

        @pl.when(kind != 2)
        def _():
            for a in range(4):
                for j in range(6):
                    tile = scratch[pl.ds(row + 96 * a + j, 16, stride=6), :]
                    look_ref[24 * t + 6 * a + j] = tile.astype(bf16)

        @pl.when(kind == 2)
        def _():
            for j in range(16):
                tile = scratch[pl.ds(row + j, 16, stride=16), :]
                look_ref[24 * t + j] = tile.astype(bf16)
            for q in range(8):
                low = scratch[pl.ds(row + 256 + q, 8, stride=16), :]
                high = scratch[pl.ds(row + 264 + q, 8, stride=16), :]
                look_ref[24 * t + 16 + q] = jnp.concatenate([low, high], 0).astype(bf16)


def tiles(x, first, count, stride):
    return jnp.concatenate([x[first + stride * i] for i in range(count)], 0)


def mm(a, b):
    return jnp.dot(a, b, preferred_element_type=f32)


def mm_t(a, b):
    return lax.dot_general(a, b, (((1,), (1,)), ((), ())), preferred_element_type=f32)


def orthogonalize(kind, base, x, wide, flat, a0, b0, wb, b1, total, emit):
    @pl.when(kind == 2)
    def _():
        def pair(i, carry):
            t = base + 48 * i
            for h in range(2):
                rows = pl.ds(pl.multiple_of(32 * i + 16 * h, 16), 16)
                for j in range(16):
                    wide[rows, 128 * j : 128 * j + 128] = x[t + 24 * h + j]
            rows = pl.ds(pl.multiple_of(512 + 16 * i, 16), 16)
            for q in range(8):
                one = x[t + 16 + q].astype(f32)
                two = x[t + 40 + q].astype(f32)
                low = jnp.concatenate([one[:8], two[:8]], 0).astype(bf16)
                high = jnp.concatenate([one[8:], two[8:]], 0).astype(bf16)
                wide[rows, 128 * q : 128 * q + 128] = low
                wide[rows, 128 * (q + 8) : 128 * (q + 8) + 128] = high
            return carry

        lax.fori_loop(0, 16, pair, 0)

    @pl.when(kind != 2)
    def _():
        def chunk(i, carry):
            columns = pl.ds(pl.multiple_of(WIDE * i, WIDE), WIDE)
            for j in range(6):
                wide[128 * j : 128 * j + 128, columns] = tiles(x, base + 96 * i + j, 16, 6).T
            return carry

        lax.fori_loop(0, 8, chunk, 0)

    parts = [slice(WIDE * n, WIDE * n + WIDE) for n in range(3)]
    iota = lax.broadcasted_iota
    square_sum = jnp.zeros((1, 1), f32)
    for part in parts:
        total[:, part] = mm_t(wide[...], wide[part, :])
        block = total[part, part]
        same = iota(jnp.int32, (WIDE, WIDE), 0) == iota(jnp.int32, (WIDE, WIDE), 1)
        square_sum = square_sum + jnp.sum(jnp.where(same, block, 0.0), keepdims=True)
    inverse = 1.0 / (jnp.sqrt(square_sum) + 1e-07)
    for part in parts:
        a0[part, :] = (total[part, :] * inverse * inverse).astype(bf16)
    for part in parts:
        square = mm(a0[...], a0[:, part])
        b0[:, part] = (coef_second * a0[:, part].astype(f32) + coef_third * square).astype(bf16)
    for part in parts:
        step = coef_first * a0[:, part].astype(f32) + mm(a0[...], b0[:, part])
        total[:, part] = coef_first * step
        wb[:, part] = step.astype(bf16)
    a1 = a0
    for part in parts:
        a1[:, part] = (total[:, part] + mm(b0[...], wb[:, part])).astype(bf16)
    for part in parts:
        square = mm(a1[...], a1[:, part])
        b1[:, part] = (coef_second * a1[:, part].astype(f32) + coef_third * square).astype(bf16)
    scale = inverse
    rest = wb
    diagonal_row = []
    diagonal_column = jnp.zeros((FF, 1), f32)
    for n, part in enumerate(parts):
        both = b0[:, part].astype(f32) + b1[:, part].astype(f32)
        step = coef_first * both + mm(b1[...], b0[:, part])
        same = iota(jnp.int32, (FF, WIDE), 0) == iota(jnp.int32, (FF, WIDE), 1) + WIDE * n
        diagonal = jnp.where(same, step, 0.0)
        diagonal_row.append(jnp.sum(diagonal, axis=0, keepdims=True))
        diagonal_column = diagonal_column + jnp.sum(diagonal, axis=1, keepdims=True)
        rest[:, part] = jnp.where(same, 0.0, step).astype(bf16)
    diagonal_row = (jnp.concatenate(diagonal_row, 1) + coef_first * coef_first) * scale
    diagonal_column = (diagonal_column + coef_first * coef_first) * scale

    @pl.when(kind != 2)
    def _():
        def chunk(i, carry):
            block = jnp.concatenate([tiles(x, base + 96 * i + j, 16, 6) for j in range(6)], 1)
            moved = mm(block, rest[...]) * scale + block.astype(f32) * diagonal_row
            for j in range(6):
                rows = pl.ds(1536 * i + j, WIDE, stride=6)
                flat[rows, :] = moved[:, 128 * j : 128 * j + 128]
            emit(i)
            return carry

        lax.fori_loop(0, 8, chunk, 0)

    @pl.when(kind == 2)
    def _():
        def chunk(i, carry):
            block = wide[:, pl.ds(pl.multiple_of(WIDE * i, WIDE), WIDE)]
            moved = mm(rest[...], block) * scale + block.astype(f32) * diagonal_column
            for h in range(2):
                panel = moved[:, 128 * h : 128 * h + 128]
                start = 2 * i + h
                for u in range(UNITS):
                    rows = pl.ds(start + 384 * u, 16, stride=16)
                    flat[rows, :] = panel[16 * u : 16 * u + 16]
                    rows = pl.ds(start + 384 * u + 256, 8, stride=16)
                    flat[rows, :] = panel[512 + 8 * u : 512 + 8 * u + 8]
            return carry

        lax.fori_loop(0, 8, chunk, 0)

        def emit_one(i, carry):
            emit(i)
            return carry

        lax.fori_loop(0, 8, emit_one, 0)


def arrivals(shard, sources, slots):
    row, column, core = shard // 8, (shard // 2) % 4, shard % 2
    found = []
    for source, (partner, second, first_hops) in zip(sources, slots):
        holder = 1 - core if partner else core
        for slot, hops in enumerate(first_hops):
            at_zero = shard_of(row - second + 4, column - hops + 4, 0)
            at_one = shard_of(row - hops + 4, column - second + 4, 1)
            found.append((source, slot, jnp.where(holder == 0, at_zero, at_one)))
    return found


def matrix_kernel(last, *refs):
    info, sources, refs = refs[0], refs[1:17], refs[17:]
    result, x, wide, flat, a0, b0, wb, b1, total, out_block, sems, more = refs
    group, shard = info[24], info[25]
    matrix = jnp.int32(2) if last else shard % 2
    first = (UNITS * matrix) // 3
    final = (UNITS * matrix + UNITS - 1) // 3
    loads = []
    for i, (source, slot, place) in enumerate(arrivals(shard, sources, PAIRS)):
        wanted = (place >= first) & (place <= final)
        target = SHARD_TILES * jnp.clip(place - first, 0, 11)
        copy = pltpu.make_async_copy(
            source.at[pl.ds(SHARD_TILES * slot, SHARD_TILES)],
            x.at[pl.ds(target, SHARD_TILES)],
            sems.at[i],
        )
        loads.append((wanted, copy))
    for wanted, copy in loads:
        pl.when(wanted)(copy.start)
    for wanted, copy in loads:
        pl.when(wanted)(copy.wait)

    kind = kind_of(info, 3 * group + matrix)
    base = MAT_TILES * matrix - SHARD_TILES * first

    def store(i):
        rows = pl.ds(pl.multiple_of(1536 * i, 1536), 1536)
        return pltpu.make_async_copy(out_block.at[rows, :], result.at[rows, :], more.at[i])

    def emit(i):
        rows = pl.ds(pl.multiple_of(1536 * i, 1536), 1536)
        out_block[rows, :] = flat[rows, :].astype(bf16)
        store(i).start()

    orthogonalize(kind, base, x, wide, flat, a0, b0, wb, b1, total, emit)
    for i in range(8):
        store(i).wait()


HOPS = (0, 1, 3, 2)
PAIRS = [(p, q, half) for p in (False, True) for q in HOPS for half in ((0, 1), (2, 3))]
QUADS = [(p, q, (0, 1, 2, 3)) for p in (False, True) for q in HOPS]


MATRIX_SCRATCH = [
    pltpu.VMEM((12 * SHARD_TILES, 16, 128), bf16),
    pltpu.VMEM((FF, D), bf16),
    pltpu.VMEM((MAT_ROWS, 128), f32),
    pltpu.VMEM((FF, FF), bf16),
    pltpu.VMEM((FF, FF), bf16),
    pltpu.VMEM((FF, FF), bf16),
    pltpu.VMEM((FF, FF), bf16),
    pltpu.VMEM((FF, FF), f32),
    pltpu.VMEM((MAT_ROWS, 128), bf16),
    pltpu.SemaphoreType.DMA((32,)),
    pltpu.SemaphoreType.DMA((8,)),
]


KEEP = 1.0 - learn_rate * weight_decay
RATE = learn_rate * 0.2 * math.sqrt(D)


def finish_kernel(info, *refs):
    mine, theirs, third, master_ref = refs[:4]
    sources = refs[4:11]
    weights, update_ref, new_ref, rest_ref, masters, moves, results, sems, stores, more = refs[11:]
    shard = info[25]
    core = shard % 2
    loads = []
    for i, (source, matrix) in enumerate(((mine, core), (theirs, 1 - core), (third, 2))):
        rows = pl.ds(pl.multiple_of(MAT_ROWS * matrix, MAT_ROWS), MAT_ROWS)
        copy = pltpu.make_async_copy(source, moves.at[rows, :], more.at[i])
        copy.start()
        loads.append(copy)
    pieces = []
    for i, (source, slot, place) in enumerate(arrivals(shard, sources, QUADS[:7])):
        rows = pl.ds(pl.multiple_of(SHARD_ROWS * place, SHARD_ROWS), SHARD_ROWS)
        copy = pltpu.make_async_copy(
            source.at[pl.ds(SHARD_ROWS * slot, SHARD_ROWS), :], masters.at[rows, :], sems.at[i]
        )
        copy.start()
        pieces.append((place, rows, copy))
    for copy in loads:
        copy.wait()
    written = []
    for i, (place, rows, copy) in enumerate(pieces):
        copy.wait()

        def weigh(n, carry):
            part = pl.ds(pl.multiple_of(SHARD_ROWS * place + 384 * n, 384), 384)
            kept = masters[part, :].astype(f32) * KEEP
            results[part, :] = (kept - RATE * moves[part, :].astype(f32)).astype(bf16)
            return carry

        lax.fori_loop(0, 3, weigh, 0)
        copy = pltpu.make_async_copy(results.at[rows, :], weights.at[rows, :], stores.at[i])
        copy.start()
        written.append(copy)
    for i, (_, _, place) in enumerate(arrivals(shard, [None], QUADS[7:])):
        rows = pl.ds(pl.multiple_of(SHARD_ROWS * place, SHARD_ROWS), SHARD_ROWS)
        rest_ref[SHARD_ROWS * i : SHARD_ROWS * i + SHARD_ROWS, :] = moves[rows, :]
    own = pl.ds(pl.multiple_of(SHARD_ROWS * shard, SHARD_ROWS), SHARD_ROWS)
    update = math.sqrt(D) * moves[own, :].astype(f32)
    update_ref[...] = update
    new_ref[...] = master_ref[...] * KEEP - learn_rate * 0.2 * update
    for copy in written:
        copy.wait()


def closing_kernel(info, _, rest, masters, weights, results, stores):
    written = []
    for i, (_, _, place) in enumerate(arrivals(info[25], [None], QUADS[7:])):
        part = slice(SHARD_ROWS * i, SHARD_ROWS * i + SHARD_ROWS)
        kept = masters[part, :].astype(f32) * KEEP
        results[part, :] = (kept - RATE * rest[part, :].astype(f32)).astype(bf16)
        rows = pl.ds(pl.multiple_of(SHARD_ROWS * place, SHARD_ROWS), SHARD_ROWS)
        copy = pltpu.make_async_copy(results.at[part, :], weights.at[rows, :], stores.at[i])
        copy.start()
        written.append(copy)
    for copy in written:
        copy.wait()


def params(mib):
    return pltpu.CompilerParams(vmem_limit_bytes=mib * MIB)


def joined(blocks, parts):
    shape = (4 // parts * blocks[0].shape[0],) + blocks[0].shape[1:]
    return pl.pallas_call(
        join_kernel,
        out_shape=(jax.ShapeDtypeStruct(shape, bf16),) * parts,
        in_specs=[VM] * 4,
        out_specs=(VM,) * parts,
        compiler_params=params(8),
    )(*blocks)


def on_device(gradient, momentum, master_weights, slot_table):
    place = jnp.stack([lax.axis_index("group"), lax.axis_index("shard")]).astype(jnp.int32)
    info = jnp.concatenate([slot_table, place])
    gradient = gradient.reshape(SHARD_ROWS, 128)
    momentum = momentum.reshape(SHARD_ROWS, 128)
    master_weights = master_weights.reshape(SHARD_ROWS, 128)

    def send(block, route):
        return lax.ppermute(block, "shard", route)

    sums, narrow = pl.pallas_call(
        opening_kernel,
        out_shape=(
            jax.ShapeDtypeStruct((32, 128), f32),
            jax.ShapeDtypeStruct((SHARD_ROWS, 128), bf16),
        ),
        in_specs=[VM, VM],
        out_specs=(VM, VM),
        compiler_params=params(8),
    )(gradient, master_weights)
    masters = [narrow] + [send(narrow, first_route(step)) for step in (1, 2, 3)]
    sums = lax.all_to_all(sums, "shard", 0, 0)
    sums = jnp.broadcast_to(jnp.sum(sums, axis=0, keepdims=True), (8, 128))
    (quad,) = joined(masters, 1)
    quad, sums = lax.optimization_barrier((quad, sums))
    sums = lax.all_to_all(sums, "group", 0, 0)

    flat_shape = jax.ShapeDtypeStruct((SHARD_ROWS, 128), f32)
    new_momentum, look = pl.pallas_call(
        look_kernel,
        out_shape=(flat_shape, jax.ShapeDtypeStruct((SHARD_TILES, 16, 128), bf16)),
        in_specs=[SM, VM, VM, VM],
        out_specs=(VM, VM),
        scratch_shapes=[pltpu.VMEM((SHARD_ROWS, 128), f32)],
        compiler_params=params(8),
    )(info, sums, gradient, momentum)

    ahead, behind = joined([look] + [send(look, first_route(step)) for step in (1, 2, 3)], 2)
    forward = [send(ahead, second_route(1)), send(behind, second_route(1))]
    backward = [send(ahead, second_route(3)), send(behind, second_route(3))]
    across = [send(forward[0], second_route(1)), send(backward[1], second_route(3))]
    early = lax.optimization_barrier([ahead, behind] + forward + backward)
    early_swapped = [send(block, swap_route()) for block in early]
    across_swapped = [send(block, swap_route()) for block in across]
    sources = early + across + early_swapped + across_swapped

    quad, sources = lax.optimization_barrier((quad, sources))
    masters = [quad, send(quad, second_route(1)), send(quad, second_route(3))]

    cost = pl.CostEstimate(flops=9_300_000_000, bytes_accessed=20_000_000, transcendentals=0)

    def orthogonalized(last):
        return pl.pallas_call(
            lambda *refs: matrix_kernel(last, *refs),
            out_shape=jax.ShapeDtypeStruct((MAT_ROWS, 128), bf16),
            in_specs=[SM] + [ANY] * 16,
            out_specs=ANY,
            scratch_shapes=MATRIX_SCRATCH,
            compiler_params=params(60),
            cost_estimate=cost,
        )(info, *sources)

    mine = orthogonalized(False)
    mine, masters = lax.optimization_barrier((mine, masters))
    theirs = send(mine, swap_route())
    across = send(masters[1], second_route(1))
    masters = masters + [across] + [send(block, swap_route()) for block in masters]
    third = orthogonalized(True)
    third, across = lax.optimization_barrier((third, across))
    last = send(across, swap_route())
    weights_shape = jax.ShapeDtypeStruct((MATS * MAT_ROWS, 128), bf16)
    quad_shape = jax.ShapeDtypeStruct((4 * SHARD_ROWS, 128), bf16)
    weights, update, new_master, rest = pl.pallas_call(
        finish_kernel,
        out_shape=(weights_shape, flat_shape, flat_shape, quad_shape),
        in_specs=[SM, ANY, ANY, ANY, VM] + [ANY] * 7,
        out_specs=(ANY, VM, VM, VM),
        scratch_shapes=[
            pltpu.VMEM((MATS * MAT_ROWS, 128), bf16),
            pltpu.VMEM((MATS * MAT_ROWS, 128), bf16),
            pltpu.VMEM((MATS * MAT_ROWS, 128), bf16),
            pltpu.SemaphoreType.DMA((28,)),
            pltpu.SemaphoreType.DMA((28,)),
            pltpu.SemaphoreType.DMA((3,)),
        ],
        compiler_params=params(56),
        cost_estimate=pl.CostEstimate(flops=10_000_000, bytes_accessed=28_000_000, transcendentals=0),
    )(info, mine, theirs, third, master_weights, *masters)
    weights = pl.pallas_call(
        closing_kernel,
        out_shape=weights_shape,
        in_specs=[SM, ANY, VM, VM],
        out_specs=ANY,
        scratch_shapes=[
            pltpu.VMEM((4 * SHARD_ROWS, 128), bf16),
            pltpu.SemaphoreType.DMA((4,)),
        ],
        input_output_aliases={1: 0},
        compiler_params=params(16),
    )(info, weights, rest, last)
    return (
        new_momentum.reshape(-1),
        update.reshape(-1),
        new_master.reshape(-1),
        weights.reshape(-1),
    )


def solution(mesh):
    in_specs = (P(("group", "shard")), P(("group", "shard")), P(("group", "shard")), P())
    out_specs = (P(("group", "shard")), P(("group", "shard")), P(("group", "shard")), P("group"))
    return jax.shard_map(
        on_device, mesh=mesh, in_specs=in_specs, out_specs=out_specs, check_vma=False
    )
```

```python
import math

import jax
import jax.numpy as jnp
from jax import lax
from jax.experimental import pallas as pl
from jax.experimental.pallas import tpu as pltpu
from jax.sharding import PartitionSpec as P

D = 2048
FF = 768
MATS = 3
UNITS = 32
SHARD_TILES = 72
SHARD_ROWS = 1152
MAT_ROWS = 12288
MAT_TILES = 768
WIDE = 256

coef_first = 3.4445
coef_second = -4.775
coef_third = 2.0315
beta_momentum = 0.95
learn_rate = 0.02
weight_decay = 0.1

f32 = jnp.float32
bf16 = jnp.bfloat16
MIB = 2**20

VM = pl.BlockSpec(memory_space=pltpu.VMEM)
SM = pl.BlockSpec(memory_space=pltpu.SMEM)
ANY = pl.BlockSpec(memory_space=pl.ANY)
HBM = pl.BlockSpec(memory_space=pltpu.HBM)


def shard_of(x, y, c):
    return (x % 4) * 8 + (y % 4) * 2 + c


def first_route(step):
    route = []
    for x in range(4):
        for y in range(4):
            route.append((shard_of(x, y, 0), shard_of(x, y + step, 0)))
            route.append((shard_of(x, y, 1), shard_of(x + step, y, 1)))
    return route


def second_route(step):
    route = []
    for x in range(4):
        for y in range(4):
            route.append((shard_of(x, y, 0), shard_of(x + step, y, 0)))
            route.append((shard_of(x, y, 1), shard_of(x, y + step, 1)))
    return route


def swap_route():
    return [(s, s ^ 1) for s in range(32)]


def kind_of(info, matrix):
    kind = jnp.int32(0)
    for m in range(24):
        kind = jnp.where(info[m] == matrix, jnp.int32(m % 3), kind)
    return kind


def opening_kernel(g_in, master_in, sums_ref, narrow_ref, g_ref, master_ref, sems):
    half = SHARD_ROWS // 2
    loads = []
    for i, (source, target) in enumerate(((g_in, g_ref), (master_in, master_ref))):
        for n in range(2):
            rows = pl.ds(half * n, half)
            copy = pltpu.make_async_copy(source.at[rows, :], target.at[rows, :], sems.at[2 * i + n])
            copy.start()
            loads.append(copy)
    total = jnp.zeros((8, 128), f32)
    for n in range(2):
        loads[n].wait()
        gradient = g_ref[half * n : half * n + half, :]
        total = total + jnp.sum((gradient * gradient).reshape(half // 8, 8, 128), axis=0)
    total = jnp.sum(jnp.sum(total, axis=0, keepdims=True), axis=1, keepdims=True)
    sums_ref[...] = jnp.broadcast_to(total, (32, 128))
    for n in range(2):
        loads[2 + n].wait()
        rows = slice(half * n, half * n + half)
        narrow_ref[rows, :] = master_ref[rows, :].astype(bf16)


def join_kernel(*refs):
    outs = refs[4:]
    length = refs[0].shape[0]
    per = 4 // len(outs)
    for i, ref in enumerate(refs[:4]):
        start = length * (i % per)
        outs[i // per][start : start + length] = ref[...]


def look_kernel(info, sums, g_ref, m_ref, nm_ref, look_ref, scratch):
    total = jnp.sum(sums[...], axis=0, keepdims=True)[:, :1]
    clip = jnp.minimum(1.0, 0.5 * math.sqrt(24 * D * FF) / jnp.sqrt(total + 1e-06))
    clipped = clip * g_ref[...]
    new_momentum = beta_momentum * m_ref[...] + clipped
    nm_ref[...] = new_momentum
    scratch[...] = clipped + beta_momentum * new_momentum
    group, shard = info[24], info[25]
    for t in range(3):
        kind = kind_of(info, 3 * group + (3 * shard + t) // UNITS)
        row = 384 * t

        @pl.when(kind != 2)
        def _():
            for a in range(4):
                for j in range(6):
                    tile = scratch[pl.ds(row + 96 * a + j, 16, stride=6), :]
                    look_ref[24 * t + 6 * a + j] = tile.astype(bf16)

        @pl.when(kind == 2)
        def _():
            for j in range(16):
                tile = scratch[pl.ds(row + j, 16, stride=16), :]
                look_ref[24 * t + j] = tile.astype(bf16)
            for q in range(8):
                low = scratch[pl.ds(row + 256 + q, 8, stride=16), :]
                high = scratch[pl.ds(row + 264 + q, 8, stride=16), :]
                look_ref[24 * t + 16 + q] = jnp.concatenate([low, high], 0).astype(bf16)


def tiles(x, first, count, stride):
    return jnp.concatenate([x[first + stride * i] for i in range(count)], 0)


def mm(a, b):
    return jnp.dot(a, b, preferred_element_type=f32)


def mm_t(a, b):
    return lax.dot_general(a, b, (((1,), (1,)), ((), ())), preferred_element_type=f32)


def orthogonalize(kind, base, x, wide, flat, a0, b0, wb, b1, total, emit):
    @pl.when(kind == 2)
    def _():
        def pair(i, carry):
            t = base + 48 * i
            for h in range(2):
                rows = pl.ds(pl.multiple_of(32 * i + 16 * h, 16), 16)
                for j in range(16):
                    wide[rows, 128 * j : 128 * j + 128] = x[t + 24 * h + j]
            rows = pl.ds(pl.multiple_of(512 + 16 * i, 16), 16)
            for q in range(8):
                one = x[t + 16 + q].astype(f32)
                two = x[t + 40 + q].astype(f32)
                low = jnp.concatenate([one[:8], two[:8]], 0).astype(bf16)
                high = jnp.concatenate([one[8:], two[8:]], 0).astype(bf16)
                wide[rows, 128 * q : 128 * q + 128] = low
                wide[rows, 128 * (q + 8) : 128 * (q + 8) + 128] = high
            return carry

        lax.fori_loop(0, 16, pair, 0)

    @pl.when(kind != 2)
    def _():
        def chunk(i, carry):
            columns = pl.ds(pl.multiple_of(WIDE * i, WIDE), WIDE)
            for j in range(6):
                wide[128 * j : 128 * j + 128, columns] = tiles(x, base + 96 * i + j, 16, 6).T
            return carry

        lax.fori_loop(0, 8, chunk, 0)

    parts = [slice(WIDE * n, WIDE * n + WIDE) for n in range(3)]
    lower = [slice(WIDE * n, FF) for n in range(3)]
    iota = lax.broadcasted_iota

    def mirror(target, n):
        for m in range(n + 1, 3):
            target[parts[n], parts[m]] = target[parts[m], parts[n]].T

    square_sum = jnp.zeros((1, 1), f32)
    same = iota(jnp.int32, (WIDE, WIDE), 0) == iota(jnp.int32, (WIDE, WIDE), 1)
    for n, part in enumerate(parts):
        total[lower[n], part] = mm_t(wide[lower[n], :], wide[part, :])
        square_sum = square_sum + jnp.sum(jnp.where(same, total[part, part], 0.0), keepdims=True)
    inverse = 1.0 / (jnp.sqrt(square_sum) + 1e-07)
    for n, part in enumerate(parts):
        a0[lower[n], part] = (total[lower[n], part] * inverse * inverse).astype(bf16)
        mirror(a0, n)
    for n, part in enumerate(parts):
        square = mm(a0[lower[n], :], a0[:, part])
        poly = coef_second * a0[lower[n], part].astype(f32) + coef_third * square
        b0[lower[n], part] = poly.astype(bf16)
        mirror(b0, n)
    for n, part in enumerate(parts):
        step = coef_first * a0[lower[n], part].astype(f32) + mm(a0[lower[n], :], b0[:, part])
        total[lower[n], part] = coef_first * step
        wb[lower[n], part] = step.astype(bf16)
        mirror(wb, n)
    a1 = a0
    for n, part in enumerate(parts):
        step = total[lower[n], part] + mm(b0[lower[n], :], wb[:, part])
        a1[lower[n], part] = step.astype(bf16)
        mirror(a1, n)
    for n, part in enumerate(parts):
        square = mm(a1[lower[n], :], a1[:, part])
        poly = coef_second * a1[lower[n], part].astype(f32) + coef_third * square
        b1[lower[n], part] = poly.astype(bf16)
        mirror(b1, n)
    scale = inverse
    rest = wb
    diagonal_row = []
    diagonal_column = []
    for n, part in enumerate(parts):
        both = b0[lower[n], part].astype(f32) + b1[lower[n], part].astype(f32)
        step = coef_first * both + mm(b1[lower[n], :], b0[:, part])
        top = jnp.where(same, step[:WIDE], 0.0)
        diagonal_row.append(jnp.sum(top, axis=0, keepdims=True))
        diagonal_column.append(jnp.sum(top, axis=1, keepdims=True))
        rest[part, part] = jnp.where(same, 0.0, step[:WIDE]).astype(bf16)
        if n < 2:
            rest[lower[n + 1], part] = step[WIDE:].astype(bf16)
        mirror(rest, n)
    diagonal_column = jnp.concatenate(diagonal_column, 0)
    diagonal_row = (jnp.concatenate(diagonal_row, 1) + coef_first * coef_first) * scale
    diagonal_column = (diagonal_column + coef_first * coef_first) * scale

    @pl.when(kind != 2)
    def _():
        def chunk(i, carry):
            block = jnp.concatenate([tiles(x, base + 192 * i + j, 32, 6) for j in range(6)], 1)
            moved = mm(block, rest[...]) * scale + block.astype(f32) * diagonal_row
            for j in range(6):
                rows = pl.ds(3072 * i + j, 2 * WIDE, stride=6)
                flat[rows, :] = moved[:, 128 * j : 128 * j + 128]
            emit(2 * i)
            emit(2 * i + 1)
            return carry

        lax.fori_loop(0, 4, chunk, 0)

    @pl.when(kind == 2)
    def _():
        def chunk(i, carry):
            block = wide[:, pl.ds(pl.multiple_of(WIDE * i, WIDE), WIDE)]
            moved = mm(rest[...], block) * scale + block.astype(f32) * diagonal_column
            for h in range(2):
                panel = moved[:, 128 * h : 128 * h + 128]
                start = 2 * i + h
                for u in range(UNITS):
                    rows = pl.ds(start + 384 * u, 16, stride=16)
                    flat[rows, :] = panel[16 * u : 16 * u + 16]
                    rows = pl.ds(start + 384 * u + 256, 8, stride=16)
                    flat[rows, :] = panel[512 + 8 * u : 512 + 8 * u + 8]
            return carry

        lax.fori_loop(0, 8, chunk, 0)

        def emit_one(i, carry):
            emit(i)
            return carry

        lax.fori_loop(0, 8, emit_one, 0)


def held_table(shard):
    n = jnp.arange(32, dtype=jnp.int32)
    partner, hops = n // 16, n % 4
    second = (n // 4) % 4
    second = jnp.where(second < 2, second, 5 - second)
    row, column, core = shard // 8, (shard // 2) % 4, shard % 2
    holder = core + partner - 2 * core * partner
    at_zero = shard_of(row - second + 4, column - hops + 4, 0)
    at_one = shard_of(row - hops + 4, column - second + 4, 1)
    return jnp.where(holder == 0, at_zero, at_one)


def held(info, partner, second, hops):
    return info[26 + 16 * int(partner) + 4 * HOPS.index(second) + hops]


def arrivals(info, sources, slots):
    found = []
    for source, (partner, second, first_hops) in zip(sources, slots):
        for slot, hops in enumerate(first_hops):
            found.append((source, slot, held(info, partner, second, hops)))
    return found


def matrix_kernel(last, *refs):
    info, sources, refs = refs[0], refs[1:17], refs[17:]
    result, x, wide, flat, a0, b0, wb, b1, total, out_block, sems, more = refs
    group, shard = info[24], info[25]
    matrix = jnp.int32(2) if last else shard % 2
    first = (UNITS * matrix) // 3
    final = (UNITS * matrix + UNITS - 1) // 3
    loads = []
    for i, (source, slot, place) in enumerate(arrivals(info, sources, PAIRS)):
        wanted = (place >= first) & (place <= final)
        target = SHARD_TILES * jnp.clip(place - first, 0, 11)
        copy = pltpu.make_async_copy(
            source.at[pl.ds(SHARD_TILES * slot, SHARD_TILES)],
            x.at[pl.ds(target, SHARD_TILES)],
            sems.at[i],
        )
        loads.append((wanted, copy))
    for wanted, copy in loads:
        pl.when(wanted)(copy.start)
    for wanted, copy in loads:
        pl.when(wanted)(copy.wait)

    kind = kind_of(info, 3 * group + matrix)
    base = MAT_TILES * matrix - SHARD_TILES * first

    def store(i):
        rows = pl.ds(pl.multiple_of(1536 * i, 1536), 1536)
        return pltpu.make_async_copy(out_block.at[rows, :], result.at[rows, :], more.at[i])

    def emit(i):
        rows = pl.ds(pl.multiple_of(1536 * i, 1536), 1536)
        out_block[rows, :] = flat[rows, :].astype(bf16)
        store(i).start()

    orthogonalize(kind, base, x, wide, flat, a0, b0, wb, b1, total, emit)
    for i in range(8):
        store(i).wait()


HOPS = (0, 1, 3, 2)
PAIRS = [(p, q, half) for p in (False, True) for q in HOPS for half in ((0, 1), (2, 3))]
QUADS = [(p, q, (0, 1, 2, 3)) for p in (False, True) for q in HOPS]


MATRIX_SCRATCH = [
    pltpu.VMEM((12 * SHARD_TILES, 16, 128), bf16),
    pltpu.VMEM((FF, D), bf16),
    pltpu.VMEM((MAT_ROWS, 128), f32),
    pltpu.VMEM((FF, FF), bf16),
    pltpu.VMEM((FF, FF), bf16),
    pltpu.VMEM((FF, FF), bf16),
    pltpu.VMEM((FF, FF), bf16),
    pltpu.VMEM((FF, FF), f32),
    pltpu.VMEM((MAT_ROWS, 128), bf16),
    pltpu.SemaphoreType.DMA((32,)),
    pltpu.SemaphoreType.DMA((8,)),
]


KEEP = 1.0 - learn_rate * weight_decay
RATE = learn_rate * 0.2 * math.sqrt(D)


def finish_kernel(info, *refs):
    mine, theirs, third, master_ref = refs[:4]
    sources = refs[4:11]
    weights, update_ref, new_ref, rest_ref, moves, results, sems, stores = refs[11:]
    shard = info[25]
    core = shard % 2
    loads = []
    for i, (source, matrix) in enumerate(((mine, core), (theirs, 1 - core), (third, 2))):
        rows = pl.ds(pl.multiple_of(MAT_ROWS * matrix, MAT_ROWS), MAT_ROWS)
        copy = pltpu.make_async_copy(source, moves.at[rows, :], sems.at[i])
        copy.start()
        loads.append(copy)
    for copy in loads:
        copy.wait()

    def rows_of(place):
        return pl.ds(pl.multiple_of(SHARD_ROWS * place, SHARD_ROWS), SHARD_ROWS)

    def store(place, i):
        rows = rows_of(place)
        return pltpu.make_async_copy(results.at[rows, :], weights.at[rows, :], stores.at[i])

    for i, (source, (partner, second, _)) in enumerate(zip(sources, QUADS)):

        def weigh(slot, carry):
            place = held(info, partner, second, slot)
            rows = rows_of(place)
            kept = source[rows_of(slot), :].astype(f32) * KEEP
            results[rows, :] = (kept - RATE * moves[rows, :].astype(f32)).astype(bf16)
            store(place, 4 * i + slot).start()
            return carry

        lax.fori_loop(0, 4, weigh, 0)

    for _, slot, place in arrivals(info, [None], QUADS[7:]):
        rest_ref[SHARD_ROWS * slot : SHARD_ROWS * slot + SHARD_ROWS, :] = moves[rows_of(place), :]
    update = math.sqrt(D) * moves[rows_of(shard), :].astype(f32)
    update_ref[...] = update
    new_ref[...] = master_ref[...] * KEEP - learn_rate * 0.2 * update
    for i, (_, slot, place) in enumerate(arrivals(info, sources, QUADS[:7])):
        store(place, i).wait()


def closing_kernel(info, _, rest, masters, weights, results, stores):
    written = []
    for i, (_, _, place) in enumerate(arrivals(info, [None], QUADS[7:])):
        part = slice(SHARD_ROWS * i, SHARD_ROWS * i + SHARD_ROWS)
        kept = masters[part, :].astype(f32) * KEEP
        results[part, :] = (kept - RATE * rest[part, :].astype(f32)).astype(bf16)
        rows = pl.ds(pl.multiple_of(SHARD_ROWS * place, SHARD_ROWS), SHARD_ROWS)
        copy = pltpu.make_async_copy(results.at[part, :], weights.at[rows, :], stores.at[i])
        copy.start()
        written.append(copy)
    for copy in written:
        copy.wait()


def params(mib):
    return pltpu.CompilerParams(vmem_limit_bytes=mib * MIB)


def joined(blocks, parts):
    shape = (4 // parts * blocks[0].shape[0],) + blocks[0].shape[1:]
    return pl.pallas_call(
        join_kernel,
        out_shape=(jax.ShapeDtypeStruct(shape, bf16),) * parts,
        in_specs=[VM] * 4,
        out_specs=(VM,) * parts,
        compiler_params=params(8),
    )(*blocks)


def on_device(gradient, momentum, master_weights, slot_table):
    group = lax.axis_index("group").astype(jnp.int32)
    shard = lax.axis_index("shard").astype(jnp.int32)
    info = jnp.concatenate([slot_table, jnp.stack([group, shard]), held_table(shard)])
    gradient = gradient.reshape(SHARD_ROWS, 128)
    momentum = momentum.reshape(SHARD_ROWS, 128)
    master_weights = master_weights.reshape(SHARD_ROWS, 128)

    def send(block, route):
        return lax.ppermute(block, "shard", route)

    sums, narrow = pl.pallas_call(
        opening_kernel,
        out_shape=(
            jax.ShapeDtypeStruct((32, 128), f32),
            jax.ShapeDtypeStruct((SHARD_ROWS, 128), bf16),
        ),
        in_specs=[HBM, HBM],
        out_specs=(VM, VM),
        scratch_shapes=[
            pltpu.VMEM((SHARD_ROWS, 128), f32),
            pltpu.VMEM((SHARD_ROWS, 128), f32),
            pltpu.SemaphoreType.DMA((4,)),
        ],
        compiler_params=params(60),
    )(gradient, master_weights)
    masters = [narrow] + [send(narrow, first_route(step)) for step in (1, 2, 3)]
    sums = lax.all_to_all(sums, "shard", 0, 0)
    sums = jnp.broadcast_to(jnp.sum(sums, axis=0, keepdims=True), (8, 128))
    (quad,) = joined(masters, 1)
    quad, sums = lax.optimization_barrier((quad, sums))
    sums = lax.all_to_all(sums, "group", 0, 0)

    flat_shape = jax.ShapeDtypeStruct((SHARD_ROWS, 128), f32)
    new_momentum, look = pl.pallas_call(
        look_kernel,
        out_shape=(flat_shape, jax.ShapeDtypeStruct((SHARD_TILES, 16, 128), bf16)),
        in_specs=[SM, VM, VM, VM],
        out_specs=(VM, VM),
        scratch_shapes=[pltpu.VMEM((SHARD_ROWS, 128), f32)],
        compiler_params=params(8),
    )(info, sums, gradient, momentum)

    ahead, behind = joined([look] + [send(look, first_route(step)) for step in (1, 2, 3)], 2)
    forward = [send(ahead, second_route(1)), send(behind, second_route(1))]
    backward = [send(ahead, second_route(3)), send(behind, second_route(3))]
    across = [send(forward[0], second_route(1)), send(backward[1], second_route(3))]
    first = lax.optimization_barrier([ahead, behind, forward[0]])[:2]
    early = first + forward + backward
    swapped = [send(block, swap_route()) for block in early]
    across, swapped = lax.optimization_barrier((across, swapped))
    sources = early + across + swapped + [send(block, swap_route()) for block in across]

    quad, sources = lax.optimization_barrier((quad, sources))
    masters = [quad, send(quad, second_route(1)), send(quad, second_route(3))]

    cost = pl.CostEstimate(flops=9_300_000_000, bytes_accessed=20_000_000, transcendentals=0)

    def orthogonalized(last):
        return pl.pallas_call(
            lambda *refs: matrix_kernel(last, *refs),
            out_shape=jax.ShapeDtypeStruct((MAT_ROWS, 128), bf16),
            in_specs=[SM] + [HBM] * 16,
            out_specs=VM if last else ANY,
            scratch_shapes=MATRIX_SCRATCH,
            compiler_params=params(29),
            cost_estimate=cost,
        )(info, *sources)

    mine = orthogonalized(False)
    mine, masters = lax.optimization_barrier((mine, masters))
    theirs = send(mine, swap_route())
    across = send(masters[1], second_route(1))
    masters = masters + [across] + [send(block, swap_route()) for block in masters]
    third = orthogonalized(True)
    third, across = lax.optimization_barrier((third, across))
    last = send(across, swap_route())
    weights_shape = jax.ShapeDtypeStruct((MATS * MAT_ROWS, 128), bf16)
    quad_shape = jax.ShapeDtypeStruct((4 * SHARD_ROWS, 128), bf16)
    weights, update, new_master, rest = pl.pallas_call(
        finish_kernel,
        out_shape=(weights_shape, flat_shape, flat_shape, quad_shape),
        in_specs=[SM] + [VM] * 11,
        out_specs=(ANY, VM, VM, VM),
        scratch_shapes=[
            pltpu.VMEM((MATS * MAT_ROWS, 128), bf16),
            pltpu.VMEM((MATS * MAT_ROWS, 128), bf16),
            pltpu.SemaphoreType.DMA((3,)),
            pltpu.SemaphoreType.DMA((28,)),
        ],
        compiler_params=params(24),
        cost_estimate=pl.CostEstimate(flops=10_000_000, bytes_accessed=28_000_000, transcendentals=0),
    )(info, mine, theirs, third, master_weights, *masters)
    weights = pl.pallas_call(
        closing_kernel,
        out_shape=weights_shape,
        in_specs=[SM, ANY, VM, VM],
        out_specs=ANY,
        scratch_shapes=[
            pltpu.VMEM((4 * SHARD_ROWS, 128), bf16),
            pltpu.SemaphoreType.DMA((4,)),
        ],
        input_output_aliases={1: 0},
        compiler_params=params(16),
    )(info, weights, rest, last)
    return (
        new_momentum.reshape(-1),
        update.reshape(-1),
        new_master.reshape(-1),
        weights.reshape(-1),
    )


def solution(mesh):
    in_specs = (P(("group", "shard")), P(("group", "shard")), P(("group", "shard")), P())
    out_specs = (P(("group", "shard")), P(("group", "shard")), P(("group", "shard")), P("group"))
    return jax.shard_map(
        on_device, mesh=mesh, in_specs=in_specs, out_specs=out_specs, check_vma=False
    )
```

```python
import math

import jax
import jax.numpy as jnp
from jax import lax
from jax.experimental import pallas as pl
from jax.experimental.pallas import tpu as pltpu
from jax.sharding import PartitionSpec as P

D = 2048
FF = 768
MATS = 3
UNITS = 32
SHARD_TILES = 72
SHARD_ROWS = 1152
MAT_ROWS = 12288
MAT_TILES = 768
WIDE = 256

coef_first = 3.4445
coef_second = -4.775
coef_third = 2.0315
beta_momentum = 0.95
learn_rate = 0.02
weight_decay = 0.1

f32 = jnp.float32
bf16 = jnp.bfloat16
MIB = 2**20

VM = pl.BlockSpec(memory_space=pltpu.VMEM)
SM = pl.BlockSpec(memory_space=pltpu.SMEM)
ANY = pl.BlockSpec(memory_space=pl.ANY)
HBM = pl.BlockSpec(memory_space=pltpu.HBM)


def shard_of(x, y, c):
    return (x % 4) * 8 + (y % 4) * 2 + c


def first_route(step):
    route = []
    for x in range(4):
        for y in range(4):
            route.append((shard_of(x, y, 0), shard_of(x, y + step, 0)))
            route.append((shard_of(x, y, 1), shard_of(x + step, y, 1)))
    return route


def second_route(step):
    route = []
    for x in range(4):
        for y in range(4):
            route.append((shard_of(x, y, 0), shard_of(x + step, y, 0)))
            route.append((shard_of(x, y, 1), shard_of(x, y + step, 1)))
    return route


def swap_route():
    return [(s, s ^ 1) for s in range(32)]


def kind_of(info, matrix):
    kind = jnp.int32(0)
    for m in range(24):
        kind = jnp.where(info[m] == matrix, jnp.int32(m % 3), kind)
    return kind


def opening_kernel(g_in, master_in, sums_ref, narrow_ref, g_ref, master_ref, sems):
    half = SHARD_ROWS // 2
    loads = []
    for i, (source, target) in enumerate(((g_in, g_ref), (master_in, master_ref))):
        for n in range(2):
            rows = pl.ds(half * n, half)
            copy = pltpu.make_async_copy(source.at[rows, :], target.at[rows, :], sems.at[2 * i + n])
            copy.start()
            loads.append(copy)
    total = jnp.zeros((8, 128), f32)
    for n in range(2):
        loads[n].wait()
        gradient = g_ref[half * n : half * n + half, :]
        total = total + jnp.sum((gradient * gradient).reshape(half // 8, 8, 128), axis=0)
    total = jnp.sum(jnp.sum(total, axis=0, keepdims=True), axis=1, keepdims=True)
    sums_ref[...] = jnp.broadcast_to(total, (32, 128))
    for n in range(2):
        loads[2 + n].wait()
        rows = slice(half * n, half * n + half)
        narrow_ref[rows, :] = master_ref[rows, :].astype(bf16)


def join_kernel(*refs):
    for out, taken in zip(refs[4:], (refs[:4], refs[:2], refs[2:4])):
        length = taken[0].shape[0]
        for i, ref in enumerate(taken):
            out[length * i : length * i + length] = ref[...]


def look_kernel(info, sums, g_ref, m_ref, nm_ref, look_ref, scratch):
    total = jnp.sum(sums[...], axis=0, keepdims=True)[:, :1]
    clip = jnp.minimum(1.0, 0.5 * math.sqrt(24 * D * FF) / jnp.sqrt(total + 1e-06))
    clipped = clip * g_ref[...]
    new_momentum = beta_momentum * m_ref[...] + clipped
    nm_ref[...] = new_momentum
    scratch[...] = clipped + beta_momentum * new_momentum
    group, shard = info[24], info[25]
    for t in range(3):
        kind = kind_of(info, 3 * group + (3 * shard + t) // UNITS)
        row = 384 * t

        @pl.when(kind != 2)
        def _():
            for a in range(4):
                for j in range(6):
                    tile = scratch[pl.ds(row + 96 * a + j, 16, stride=6), :]
                    look_ref[24 * t + 6 * a + j] = tile.astype(bf16)

        @pl.when(kind == 2)
        def _():
            for j in range(16):
                tile = scratch[pl.ds(row + j, 16, stride=16), :]
                look_ref[24 * t + j] = tile.astype(bf16)
            for q in range(8):
                low = scratch[pl.ds(row + 256 + q, 8, stride=16), :]
                high = scratch[pl.ds(row + 264 + q, 8, stride=16), :]
                look_ref[24 * t + 16 + q] = jnp.concatenate([low, high], 0).astype(bf16)


def tiles(x, first, count, stride):
    return jnp.concatenate([x[first + stride * i] for i in range(count)], 0)


def mm(a, b):
    return jnp.dot(a, b, preferred_element_type=f32)


def mm_t(a, b):
    return lax.dot_general(a, b, (((1,), (1,)), ((), ())), preferred_element_type=f32)


def orthogonalize(kind, base, x, wide, flat, a0, b0, wb, b1, total, emit):
    @pl.when(kind == 2)
    def _():
        def pair(i, carry):
            t = base + 48 * i
            for h in range(2):
                rows = pl.ds(pl.multiple_of(32 * i + 16 * h, 16), 16)
                for j in range(16):
                    wide[rows, 128 * j : 128 * j + 128] = x[t + 24 * h + j]
            rows = pl.ds(pl.multiple_of(512 + 16 * i, 16), 16)
            for q in range(8):
                one = x[t + 16 + q].astype(f32)
                two = x[t + 40 + q].astype(f32)
                low = jnp.concatenate([one[:8], two[:8]], 0).astype(bf16)
                high = jnp.concatenate([one[8:], two[8:]], 0).astype(bf16)
                wide[rows, 128 * q : 128 * q + 128] = low
                wide[rows, 128 * (q + 8) : 128 * (q + 8) + 128] = high
            return carry

        lax.fori_loop(0, 16, pair, 0)

    @pl.when(kind != 2)
    def _():
        def chunk(i, carry):
            columns = pl.ds(pl.multiple_of(WIDE * i, WIDE), WIDE)
            for j in range(6):
                wide[128 * j : 128 * j + 128, columns] = tiles(x, base + 96 * i + j, 16, 6).T
            return carry

        lax.fori_loop(0, 8, chunk, 0)

    parts = [slice(WIDE * n, WIDE * n + WIDE) for n in range(3)]
    lower = [slice(WIDE * n, FF) for n in range(3)]
    iota = lax.broadcasted_iota

    def mirror(target, n):
        for m in range(n + 1, 3):
            target[parts[n], parts[m]] = target[parts[m], parts[n]].T

    square_sum = jnp.zeros((1, 1), f32)
    same = iota(jnp.int32, (WIDE, WIDE), 0) == iota(jnp.int32, (WIDE, WIDE), 1)
    for n, part in enumerate(parts):
        total[lower[n], part] = mm_t(wide[lower[n], :], wide[part, :])
        square_sum = square_sum + jnp.sum(jnp.where(same, total[part, part], 0.0), keepdims=True)
    inverse = 1.0 / (jnp.sqrt(square_sum) + 1e-07)
    for n, part in enumerate(parts):
        a0[lower[n], part] = (total[lower[n], part] * inverse * inverse).astype(bf16)
        mirror(a0, n)
    for n, part in enumerate(parts):
        square = mm(a0[lower[n], :], a0[:, part])
        poly = coef_second * a0[lower[n], part].astype(f32) + coef_third * square
        b0[lower[n], part] = poly.astype(bf16)
        mirror(b0, n)
    for n, part in enumerate(parts):
        step = coef_first * a0[lower[n], part].astype(f32) + mm(a0[lower[n], :], b0[:, part])
        total[lower[n], part] = coef_first * step
        wb[lower[n], part] = step.astype(bf16)
        mirror(wb, n)
    a1 = a0
    for n, part in enumerate(parts):
        step = total[lower[n], part] + mm(b0[lower[n], :], wb[:, part])
        a1[lower[n], part] = step.astype(bf16)
        mirror(a1, n)
    for n, part in enumerate(parts):
        square = mm(a1[lower[n], :], a1[:, part])
        poly = coef_second * a1[lower[n], part].astype(f32) + coef_third * square
        b1[lower[n], part] = poly.astype(bf16)
        mirror(b1, n)
    scale = inverse
    rest = wb
    diagonal_row = []
    diagonal_column = []
    for n, part in enumerate(parts):
        both = b0[lower[n], part].astype(f32) + b1[lower[n], part].astype(f32)
        step = coef_first * both + mm(b1[lower[n], :], b0[:, part])
        top = jnp.where(same, step[:WIDE], 0.0)
        diagonal_row.append(jnp.sum(top, axis=0, keepdims=True))
        diagonal_column.append(jnp.sum(top, axis=1, keepdims=True))
        rest[part, part] = jnp.where(same, 0.0, step[:WIDE]).astype(bf16)
        if n < 2:
            rest[lower[n + 1], part] = step[WIDE:].astype(bf16)
        mirror(rest, n)
    diagonal_column = jnp.concatenate(diagonal_column, 0)
    diagonal_row = (jnp.concatenate(diagonal_row, 1) + coef_first * coef_first) * scale
    diagonal_column = (diagonal_column + coef_first * coef_first) * scale

    @pl.when(kind != 2)
    def _():
        def chunk(i, carry):
            block = jnp.concatenate([tiles(x, base + 192 * i + j, 32, 6) for j in range(6)], 1)
            moved = mm(block, rest[...]) * scale + block.astype(f32) * diagonal_row
            for j in range(6):
                rows = pl.ds(3072 * i + j, 2 * WIDE, stride=6)
                flat[rows, :] = moved[:, 128 * j : 128 * j + 128]
            emit(2 * i)
            emit(2 * i + 1)
            return carry

        lax.fori_loop(0, 4, chunk, 0)

    @pl.when(kind == 2)
    def _():
        def chunk(i, carry):
            block = wide[:, pl.ds(pl.multiple_of(WIDE * i, WIDE), WIDE)]
            moved = mm(rest[...], block) * scale + block.astype(f32) * diagonal_column
            for h in range(2):
                panel = moved[:, 128 * h : 128 * h + 128]
                start = 2 * i + h
                for u in range(UNITS):
                    rows = pl.ds(start + 384 * u, 16, stride=16)
                    flat[rows, :] = panel[16 * u : 16 * u + 16]
                    rows = pl.ds(start + 384 * u + 256, 8, stride=16)
                    flat[rows, :] = panel[512 + 8 * u : 512 + 8 * u + 8]
            return carry

        lax.fori_loop(0, 8, chunk, 0)

        def emit_one(i, carry):
            emit(i)
            return carry

        lax.fori_loop(0, 8, emit_one, 0)


def held_table(shard):
    n = jnp.arange(32, dtype=jnp.int32)
    partner, hops = n // 16, n % 4
    second = (n // 4) % 4
    second = jnp.where(second < 2, second, 5 - second)
    row, column, core = shard // 8, (shard // 2) % 4, shard % 2
    holder = core + partner - 2 * core * partner
    at_zero = shard_of(row - second + 4, column - hops + 4, 0)
    at_one = shard_of(row - hops + 4, column - second + 4, 1)
    return jnp.where(holder == 0, at_zero, at_one)


def held(info, partner, second, hops):
    return info[26 + 16 * int(partner) + 4 * HOPS.index(second) + hops]


def arrivals(info, sources, slots):
    found = []
    for source, (partner, second, first_hops) in zip(sources, slots):
        for slot, hops in enumerate(first_hops):
            found.append((source, slot, held(info, partner, second, hops)))
    return found


def matrix_kernel(last, *refs):
    info, sources, refs = refs[0], refs[1:15], refs[15:]
    result, x, wide, flat, a0, b0, wb, b1, total, out_block, sems, more = refs
    group, shard = info[24], info[25]
    matrix = jnp.int32(2) if last else shard % 2
    first = (UNITS * matrix) // 3
    final = (UNITS * matrix + UNITS - 1) // 3
    loads = []
    for i, (source, slot, place) in enumerate(arrivals(info, sources, BLOCKS)):
        wanted = (place >= first) & (place <= final)
        target = SHARD_TILES * jnp.clip(place - first, 0, 11)
        copy = pltpu.make_async_copy(
            source.at[pl.ds(SHARD_TILES * slot, SHARD_TILES)],
            x.at[pl.ds(target, SHARD_TILES)],
            sems.at[i],
        )
        loads.append((wanted, copy))
    for wanted, copy in loads:
        pl.when(wanted)(copy.start)
    for wanted, copy in loads:
        pl.when(wanted)(copy.wait)

    kind = kind_of(info, 3 * group + matrix)
    base = MAT_TILES * matrix - SHARD_TILES * first

    def store(i):
        rows = pl.ds(pl.multiple_of(1536 * i, 1536), 1536)
        return pltpu.make_async_copy(out_block.at[rows, :], result.at[rows, :], more.at[i])

    def emit(i):
        rows = pl.ds(pl.multiple_of(1536 * i, 1536), 1536)
        out_block[rows, :] = flat[rows, :].astype(bf16)
        store(i).start()

    orthogonalize(kind, base, x, wide, flat, a0, b0, wb, b1, total, emit)
    for i in range(8):
        store(i).wait()


HOPS = (0, 1, 3, 2)
BLOCKS = [
    (p, q, dp)
    for p in (False, True)
    for q, dp in ((0, (0, 1, 2, 3)), (1, (0, 1)), (3, (2, 3)), (1, (2, 3)), (3, (0, 1)))
]
BLOCKS = BLOCKS[:5] + [(False, 2, (0, 1)), (False, 2, (2, 3))] + BLOCKS[5:]
BLOCKS = BLOCKS + [(True, 2, (0, 1)), (True, 2, (2, 3))]
QUADS = [(p, q, (0, 1, 2, 3)) for p in (False, True) for q in HOPS]


MATRIX_SCRATCH = [
    pltpu.VMEM((12 * SHARD_TILES, 16, 128), bf16),
    pltpu.VMEM((FF, D), bf16),
    pltpu.VMEM((MAT_ROWS, 128), f32),
    pltpu.VMEM((FF, FF), bf16),
    pltpu.VMEM((FF, FF), bf16),
    pltpu.VMEM((FF, FF), bf16),
    pltpu.VMEM((FF, FF), bf16),
    pltpu.VMEM((FF, FF), f32),
    pltpu.VMEM((MAT_ROWS, 128), bf16),
    pltpu.SemaphoreType.DMA((32,)),
    pltpu.SemaphoreType.DMA((8,)),
]


KEEP = 1.0 - learn_rate * weight_decay
RATE = learn_rate * 0.2 * math.sqrt(D)


def finish_kernel(info, *refs):
    mine, theirs, third, master_ref = refs[:4]
    sources = refs[4:11]
    weights, update_ref, new_ref, rest_ref, moves, results, sems, stores = refs[11:]
    shard = info[25]
    core = shard % 2
    loads = []
    for i, (source, matrix) in enumerate(((mine, core), (theirs, 1 - core), (third, 2))):
        rows = pl.ds(pl.multiple_of(MAT_ROWS * matrix, MAT_ROWS), MAT_ROWS)
        copy = pltpu.make_async_copy(source, moves.at[rows, :], sems.at[i])
        copy.start()
        loads.append(copy)
    for copy in loads:
        copy.wait()

    def rows_of(place):
        return pl.ds(pl.multiple_of(SHARD_ROWS * place, SHARD_ROWS), SHARD_ROWS)

    def store(place, i):
        rows = rows_of(place)
        return pltpu.make_async_copy(results.at[rows, :], weights.at[rows, :], stores.at[i])

    for i, (source, (partner, second, _)) in enumerate(zip(sources, QUADS)):

        def weigh(slot, carry):
            place = held(info, partner, second, slot)
            rows = rows_of(place)
            kept = source[rows_of(slot), :].astype(f32) * KEEP
            results[rows, :] = (kept - RATE * moves[rows, :].astype(f32)).astype(bf16)
            store(place, 4 * i + slot).start()
            return carry

        lax.fori_loop(0, 4, weigh, 0)

    for _, slot, place in arrivals(info, [None], QUADS[7:]):
        rest_ref[SHARD_ROWS * slot : SHARD_ROWS * slot + SHARD_ROWS, :] = moves[rows_of(place), :]
    update = math.sqrt(D) * moves[rows_of(shard), :].astype(f32)
    update_ref[...] = update
    new_ref[...] = master_ref[...] * KEEP - learn_rate * 0.2 * update
    for i, (_, slot, place) in enumerate(arrivals(info, sources, QUADS[:7])):
        store(place, i).wait()


def closing_kernel(info, _, rest, masters, weights, results, stores):
    written = []
    for i, (_, _, place) in enumerate(arrivals(info, [None], QUADS[7:])):
        part = slice(SHARD_ROWS * i, SHARD_ROWS * i + SHARD_ROWS)
        kept = masters[part, :].astype(f32) * KEEP
        results[part, :] = (kept - RATE * rest[part, :].astype(f32)).astype(bf16)
        rows = pl.ds(pl.multiple_of(SHARD_ROWS * place, SHARD_ROWS), SHARD_ROWS)
        copy = pltpu.make_async_copy(results.at[part, :], weights.at[rows, :], stores.at[i])
        copy.start()
        written.append(copy)
    for copy in written:
        copy.wait()


def params(mib):
    return pltpu.CompilerParams(vmem_limit_bytes=mib * MIB)


def joined(blocks, parts):
    lengths = [4 * blocks[0].shape[0]] + [2 * blocks[0].shape[0]] * (parts - 1)
    return pl.pallas_call(
        join_kernel,
        out_shape=tuple(jax.ShapeDtypeStruct((n,) + blocks[0].shape[1:], bf16) for n in lengths),
        in_specs=[VM] * 4,
        out_specs=(VM,) * parts,
        compiler_params=params(8),
    )(*blocks)


def on_device(gradient, momentum, master_weights, slot_table):
    group = lax.axis_index("group").astype(jnp.int32)
    shard = lax.axis_index("shard").astype(jnp.int32)
    info = jnp.concatenate([slot_table, jnp.stack([group, shard]), held_table(shard)])
    gradient = gradient.reshape(SHARD_ROWS, 128)
    momentum = momentum.reshape(SHARD_ROWS, 128)
    master_weights = master_weights.reshape(SHARD_ROWS, 128)

    def send(block, route):
        return lax.ppermute(block, "shard", route)

    sums, narrow = pl.pallas_call(
        opening_kernel,
        out_shape=(
            jax.ShapeDtypeStruct((32, 128), f32),
            jax.ShapeDtypeStruct((SHARD_ROWS, 128), bf16),
        ),
        in_specs=[HBM, HBM],
        out_specs=(VM, VM),
        scratch_shapes=[
            pltpu.VMEM((SHARD_ROWS, 128), f32),
            pltpu.VMEM((SHARD_ROWS, 128), f32),
            pltpu.SemaphoreType.DMA((4,)),
        ],
        compiler_params=params(60),
    )(gradient, master_weights)
    masters = [narrow] + [send(narrow, first_route(step)) for step in (1, 2, 3)]
    sums = lax.all_to_all(sums, "shard", 0, 0)
    sums = jnp.broadcast_to(jnp.sum(sums, axis=0, keepdims=True), (8, 128))
    (quad,) = joined(masters, 1)
    quad, sums = lax.optimization_barrier((quad, sums))
    sums = lax.all_to_all(sums, "group", 0, 0)

    flat_shape = jax.ShapeDtypeStruct((SHARD_ROWS, 128), f32)
    new_momentum, look = pl.pallas_call(
        look_kernel,
        out_shape=(flat_shape, jax.ShapeDtypeStruct((SHARD_TILES, 16, 128), bf16)),
        in_specs=[SM, VM, VM, VM],
        out_specs=(VM, VM),
        scratch_shapes=[pltpu.VMEM((SHARD_ROWS, 128), f32)],
        compiler_params=params(8),
    )(info, sums, gradient, momentum)

    whole, ahead, behind = joined([look] + [send(look, first_route(step)) for step in (1, 2, 3)], 3)
    forward = [send(ahead, second_route(1)), send(behind, second_route(1))]
    backward = [send(ahead, second_route(3)), send(behind, second_route(3))]
    across = [send(forward[0], second_route(1)), send(backward[1], second_route(3))]
    whole, forward[0] = lax.optimization_barrier((whole, forward[0]))
    early = [whole, forward[0], backward[1], forward[1], backward[0]]
    swapped = [send(block, swap_route()) for block in early]
    across, swapped = lax.optimization_barrier((across, swapped))
    sources = early + across + swapped + [send(block, swap_route()) for block in across]

    quad, sources = lax.optimization_barrier((quad, sources))
    masters = [quad, send(quad, second_route(1)), send(quad, second_route(3))]

    cost = pl.CostEstimate(flops=9_300_000_000, bytes_accessed=20_000_000, transcendentals=0)

    def orthogonalized(last):
        return pl.pallas_call(
            lambda *refs: matrix_kernel(last, *refs),
            out_shape=jax.ShapeDtypeStruct((MAT_ROWS, 128), bf16),
            in_specs=[SM] + [HBM] * 14,
            out_specs=VM if last else ANY,
            scratch_shapes=MATRIX_SCRATCH,
            compiler_params=params(29),
            cost_estimate=cost,
        )(info, *sources)

    mine = orthogonalized(False)
    mine, masters = lax.optimization_barrier((mine, masters))
    theirs = send(mine, swap_route())
    across = send(masters[1], second_route(1))
    masters = masters + [across] + [send(block, swap_route()) for block in masters]
    third = orthogonalized(True)
    third, across = lax.optimization_barrier((third, across))
    last = send(across, swap_route())
    weights_shape = jax.ShapeDtypeStruct((MATS * MAT_ROWS, 128), bf16)
    quad_shape = jax.ShapeDtypeStruct((4 * SHARD_ROWS, 128), bf16)
    weights, update, new_master, rest = pl.pallas_call(
        finish_kernel,
        out_shape=(weights_shape, flat_shape, flat_shape, quad_shape),
        in_specs=[SM] + [VM] * 11,
        out_specs=(ANY, VM, VM, VM),
        scratch_shapes=[
            pltpu.VMEM((MATS * MAT_ROWS, 128), bf16),
            pltpu.VMEM((MATS * MAT_ROWS, 128), bf16),
            pltpu.SemaphoreType.DMA((3,)),
            pltpu.SemaphoreType.DMA((28,)),
        ],
        compiler_params=params(24),
        cost_estimate=pl.CostEstimate(flops=10_000_000, bytes_accessed=28_000_000, transcendentals=0),
    )(info, mine, theirs, third, master_weights, *masters)
    weights = pl.pallas_call(
        closing_kernel,
        out_shape=weights_shape,
        in_specs=[SM, ANY, VM, VM],
        out_specs=ANY,
        scratch_shapes=[
            pltpu.VMEM((4 * SHARD_ROWS, 128), bf16),
            pltpu.SemaphoreType.DMA((4,)),
        ],
        input_output_aliases={1: 0},
        compiler_params=params(16),
    )(info, weights, rest, last)
    return (
        new_momentum.reshape(-1),
        update.reshape(-1),
        new_master.reshape(-1),
        weights.reshape(-1),
    )


def solution(mesh):
    in_specs = (P(("group", "shard")), P(("group", "shard")), P(("group", "shard")), P())
    out_specs = (P(("group", "shard")), P(("group", "shard")), P(("group", "shard")), P("group"))
    return jax.shard_map(
        on_device, mesh=mesh, in_specs=in_specs, out_specs=out_specs, check_vma=False
    )
```

```python
import math

import jax
import jax.numpy as jnp
from jax import lax
from jax.experimental import pallas as pl
from jax.experimental.pallas import tpu as pltpu
from jax.sharding import PartitionSpec as P

D = 2048
FF = 768
MATS = 3
UNITS = 32
SHARD_TILES = 72
SHARD_ROWS = 1152
MAT_ROWS = 12288
MAT_TILES = 768
WIDE = 256

coef_first = 3.4445
coef_second = -4.775
coef_third = 2.0315
beta_momentum = 0.95
learn_rate = 0.02
weight_decay = 0.1

f32 = jnp.float32
bf16 = jnp.bfloat16
MIB = 2**20

VM = pl.BlockSpec(memory_space=pltpu.VMEM)
SM = pl.BlockSpec(memory_space=pltpu.SMEM)
ANY = pl.BlockSpec(memory_space=pl.ANY)
HBM = pl.BlockSpec(memory_space=pltpu.HBM)


def shard_of(x, y, c):
    return (x % 4) * 8 + (y % 4) * 2 + c


def first_route(step):
    route = []
    for x in range(4):
        for y in range(4):
            route.append((shard_of(x, y, 0), shard_of(x, y + step, 0)))
            route.append((shard_of(x, y, 1), shard_of(x + step, y, 1)))
    return route


def second_route(step):
    route = []
    for x in range(4):
        for y in range(4):
            route.append((shard_of(x, y, 0), shard_of(x + step, y, 0)))
            route.append((shard_of(x, y, 1), shard_of(x, y + step, 1)))
    return route


def swap_route():
    return [(s, s ^ 1) for s in range(32)]


def kind_of(info, matrix):
    kind = jnp.int32(0)
    for m in range(24):
        kind = jnp.where(info[m] == matrix, jnp.int32(m % 3), kind)
    return kind


def opening_kernel(g_in, master_in, sums_ref, narrow_ref, g_ref, master_ref, sems):
    half = SHARD_ROWS // 2
    loads = []
    for i, (source, target) in enumerate(((g_in, g_ref), (master_in, master_ref))):
        for n in range(2):
            rows = pl.ds(half * n, half)
            copy = pltpu.make_async_copy(source.at[rows, :], target.at[rows, :], sems.at[2 * i + n])
            copy.start()
            loads.append(copy)
    total = jnp.zeros((8, 128), f32)
    for n in range(2):
        loads[n].wait()
        gradient = g_ref[half * n : half * n + half, :]
        total = total + jnp.sum((gradient * gradient).reshape(half // 8, 8, 128), axis=0)
    total = jnp.sum(jnp.sum(total, axis=0, keepdims=True), axis=1, keepdims=True)
    sums_ref[...] = jnp.broadcast_to(total, (32, 128))
    for n in range(2):
        loads[2 + n].wait()
        rows = slice(half * n, half * n + half)
        narrow_ref[rows, :] = master_ref[rows, :].astype(bf16)


def join_kernel(*refs):
    for out, taken in zip(refs[4:], (refs[:4], refs[:2], refs[2:4])):
        length = taken[0].shape[0]
        for i, ref in enumerate(taken):
            out[length * i : length * i + length] = ref[...]


def look_kernel(info, sums, g_ref, m_ref, nm_ref, look_ref, scratch):
    total = jnp.sum(sums[...], axis=0, keepdims=True)[:, :1]
    clip = jnp.minimum(1.0, 0.5 * math.sqrt(24 * D * FF) / jnp.sqrt(total + 1e-06))
    clipped = clip * g_ref[...]
    new_momentum = beta_momentum * m_ref[...] + clipped
    nm_ref[...] = new_momentum
    scratch[...] = clipped + beta_momentum * new_momentum
    group, shard = info[24], info[25]
    for t in range(3):
        kind = kind_of(info, 3 * group + (3 * shard + t) // UNITS)
        row = 384 * t

        @pl.when(kind != 2)
        def _():
            for a in range(4):
                for j in range(6):
                    tile = scratch[pl.ds(row + 96 * a + j, 16, stride=6), :]
                    look_ref[24 * t + 6 * a + j] = tile.astype(bf16)

        @pl.when(kind == 2)
        def _():
            for j in range(16):
                tile = scratch[pl.ds(row + j, 16, stride=16), :]
                look_ref[24 * t + j] = tile.astype(bf16)
            for q in range(8):
                low = scratch[pl.ds(row + 256 + q, 8, stride=16), :]
                high = scratch[pl.ds(row + 264 + q, 8, stride=16), :]
                look_ref[24 * t + 16 + q] = jnp.concatenate([low, high], 0).astype(bf16)


def tiles(x, first, count, stride):
    return jnp.concatenate([x[first + stride * i] for i in range(count)], 0)


def mm(a, b):
    return jnp.dot(a, b, preferred_element_type=f32)


def mm_t(a, b):
    return lax.dot_general(a, b, (((1,), (1,)), ((), ())), preferred_element_type=f32)


def orthogonalize(kind, base, x, wide, flat, a0, b0, wb, b1, total, emit):
    @pl.when(kind == 2)
    def _():
        def pair(i, carry):
            t = base + 48 * i
            for h in range(2):
                rows = pl.ds(pl.multiple_of(32 * i + 16 * h, 16), 16)
                for j in range(16):
                    wide[rows, 128 * j : 128 * j + 128] = x[t + 24 * h + j]
            rows = pl.ds(pl.multiple_of(512 + 16 * i, 16), 16)
            for q in range(8):
                one = x[t + 16 + q].astype(f32)
                two = x[t + 40 + q].astype(f32)
                low = jnp.concatenate([one[:8], two[:8]], 0).astype(bf16)
                high = jnp.concatenate([one[8:], two[8:]], 0).astype(bf16)
                wide[rows, 128 * q : 128 * q + 128] = low
                wide[rows, 128 * (q + 8) : 128 * (q + 8) + 128] = high
            return carry

        lax.fori_loop(0, 16, pair, 0)

    @pl.when(kind != 2)
    def _():
        def chunk(i, carry):
            columns = pl.ds(pl.multiple_of(WIDE * i, WIDE), WIDE)
            for j in range(6):
                wide[128 * j : 128 * j + 128, columns] = tiles(x, base + 96 * i + j, 16, 6).T
            return carry

        lax.fori_loop(0, 8, chunk, 0)

    parts = [slice(WIDE * n, WIDE * n + WIDE) for n in range(3)]
    lower = [slice(WIDE * n, FF) for n in range(3)]
    iota = lax.broadcasted_iota

    def mirror(target, n):
        for m in range(n + 1, 3):
            target[parts[n], parts[m]] = target[parts[m], parts[n]].T

    square_sum = jnp.zeros((1, 1), f32)
    same = iota(jnp.int32, (WIDE, WIDE), 0) == iota(jnp.int32, (WIDE, WIDE), 1)
    for n, part in enumerate(parts):
        total[lower[n], part] = mm_t(wide[lower[n], :], wide[part, :])
        square_sum = square_sum + jnp.sum(jnp.where(same, total[part, part], 0.0), keepdims=True)
    inverse = 1.0 / (jnp.sqrt(square_sum) + 1e-07)
    for n, part in enumerate(parts):
        a0[lower[n], part] = (total[lower[n], part] * inverse * inverse).astype(bf16)
        mirror(a0, n)
    for n, part in enumerate(parts):
        square = mm(a0[lower[n], :], a0[:, part])
        poly = coef_second * a0[lower[n], part].astype(f32) + coef_third * square
        b0[lower[n], part] = poly.astype(bf16)
        mirror(b0, n)
    for n, part in enumerate(parts):
        step = coef_first * a0[lower[n], part].astype(f32) + mm(a0[lower[n], :], b0[:, part])
        total[lower[n], part] = coef_first * step
        wb[lower[n], part] = step.astype(bf16)
        mirror(wb, n)
    a1 = a0
    for n, part in enumerate(parts):
        step = total[lower[n], part] + mm(b0[lower[n], :], wb[:, part])
        a1[lower[n], part] = step.astype(bf16)
        mirror(a1, n)
    for n, part in enumerate(parts):
        square = mm(a1[lower[n], :], a1[:, part])
        poly = coef_second * a1[lower[n], part].astype(f32) + coef_third * square
        b1[lower[n], part] = poly.astype(bf16)
        mirror(b1, n)
    scale = inverse
    rest = wb
    diagonal_row = []
    diagonal_column = []
    for n, part in enumerate(parts):
        both = b0[lower[n], part].astype(f32) + b1[lower[n], part].astype(f32)
        step = coef_first * both + mm(b1[lower[n], :], b0[:, part])
        top = jnp.where(same, step[:WIDE], 0.0)
        diagonal_row.append(jnp.sum(top, axis=0, keepdims=True))
        diagonal_column.append(jnp.sum(top, axis=1, keepdims=True))
        rest[part, part] = (jnp.where(same, 0.0, step[:WIDE]) * scale).astype(bf16)
        if n < 2:
            rest[lower[n + 1], part] = (step[WIDE:] * scale).astype(bf16)
        mirror(rest, n)
    diagonal_column = jnp.concatenate(diagonal_column, 0)
    diagonal_row = (jnp.concatenate(diagonal_row, 1) + coef_first * coef_first) * scale
    diagonal_column = (diagonal_column + coef_first * coef_first) * scale

    @pl.when(kind != 2)
    def _():
        def chunk(i, carry):
            block = jnp.concatenate([tiles(x, base + 192 * i + j, 32, 6) for j in range(6)], 1)
            moved = mm(block, rest[...]) + block.astype(f32) * diagonal_row
            for j in range(6):
                rows = pl.ds(3072 * i + j, 2 * WIDE, stride=6)
                flat[rows, :] = moved[:, 128 * j : 128 * j + 128]
            emit(2 * i)
            emit(2 * i + 1)
            return carry

        lax.fori_loop(0, 4, chunk, 0)

    @pl.when(kind == 2)
    def _():
        def chunk(i, carry):
            block = wide[:, pl.ds(pl.multiple_of(WIDE * i, WIDE), WIDE)]
            moved = mm(rest[...], block) + block.astype(f32) * diagonal_column
            for h in range(2):
                panel = moved[:, 128 * h : 128 * h + 128]
                start = 2 * i + h
                for u in range(UNITS):
                    rows = pl.ds(start + 384 * u, 16, stride=16)
                    flat[rows, :] = panel[16 * u : 16 * u + 16]
                    rows = pl.ds(start + 384 * u + 256, 8, stride=16)
                    flat[rows, :] = panel[512 + 8 * u : 512 + 8 * u + 8]
            return carry

        lax.fori_loop(0, 8, chunk, 0)

        def emit_one(i, carry):
            emit(i)
            return carry

        lax.fori_loop(0, 8, emit_one, 0)


def held_table(shard):
    n = jnp.arange(32, dtype=jnp.int32)
    partner, hops = n // 16, n % 4
    second = (n // 4) % 4
    second = jnp.where(second < 2, second, 5 - second)
    row, column, core = shard // 8, (shard // 2) % 4, shard % 2
    holder = core + partner - 2 * core * partner
    at_zero = shard_of(row - second + 4, column - hops + 4, 0)
    at_one = shard_of(row - hops + 4, column - second + 4, 1)
    return jnp.where(holder == 0, at_zero, at_one)


def held(info, partner, second, hops):
    return info[26 + 16 * int(partner) + 4 * HOPS.index(second) + hops]


def arrivals(info, sources, slots):
    found = []
    for source, (partner, second, first_hops) in zip(sources, slots):
        for slot, hops in enumerate(first_hops):
            found.append((source, slot, held(info, partner, second, hops)))
    return found


def matrix_kernel(last, *refs):
    info, sources, refs = refs[0], refs[1:15], refs[15:]
    result, x, wide, flat, a0, b0, wb, b1, total, sems = refs
    group, shard = info[24], info[25]
    matrix = jnp.int32(2) if last else shard % 2
    first = (UNITS * matrix) // 3
    final = (UNITS * matrix + UNITS - 1) // 3
    loads = []
    for i, (source, slot, place) in enumerate(arrivals(info, sources, BLOCKS)):
        wanted = (place >= first) & (place <= final)
        target = SHARD_TILES * jnp.clip(place - first, 0, 11)
        copy = pltpu.make_async_copy(
            source.at[pl.ds(SHARD_TILES * slot, SHARD_TILES)],
            x.at[pl.ds(target, SHARD_TILES)],
            sems.at[i],
        )
        loads.append((wanted, copy))
    for wanted, copy in loads:
        pl.when(wanted)(copy.start)
    for wanted, copy in loads:
        pl.when(wanted)(copy.wait)

    kind = kind_of(info, 3 * group + matrix)
    base = MAT_TILES * matrix - SHARD_TILES * first

    def emit(i):
        rows = pl.ds(pl.multiple_of(1536 * i, 1536), 1536)
        result[rows, :] = flat[rows, :].astype(bf16)

    orthogonalize(kind, base, x, wide, flat, a0, b0, wb, b1, total, emit)


HOPS = (0, 1, 3, 2)
BLOCKS = [
    (p, q, dp)
    for p in (False, True)
    for q, dp in ((0, (0, 1, 2, 3)), (1, (0, 1)), (3, (2, 3)), (1, (2, 3)), (3, (0, 1)))
]
BLOCKS = BLOCKS[:5] + [(False, 2, (0, 1)), (False, 2, (2, 3))] + BLOCKS[5:]
BLOCKS = BLOCKS + [(True, 2, (0, 1)), (True, 2, (2, 3))]
QUADS = [(p, q, (0, 1, 2, 3)) for p in (False, True) for q in HOPS]


MATRIX_SCRATCH = [
    pltpu.VMEM((12 * SHARD_TILES, 16, 128), bf16),
    pltpu.VMEM((FF, D), bf16),
    pltpu.VMEM((MAT_ROWS, 128), f32),
    pltpu.VMEM((FF, FF), bf16),
    pltpu.VMEM((FF, FF), bf16),
    pltpu.VMEM((FF, FF), bf16),
    pltpu.VMEM((FF, FF), bf16),
    pltpu.VMEM((FF, FF), f32),
    pltpu.SemaphoreType.DMA((32,)),
]


KEEP = 1.0 - learn_rate * weight_decay
RATE = learn_rate * 0.2 * math.sqrt(D)


def finish_kernel(info, *refs):
    mine, theirs, third, master_ref = refs[:4]
    sources = refs[4:11]
    weights, update_ref, new_ref, rest_ref, moves, results, sems, stores = refs[11:]
    shard = info[25]
    core = shard % 2
    loads = []
    for i, (source, matrix) in enumerate(((mine, core), (theirs, 1 - core), (third, 2))):
        rows = pl.ds(pl.multiple_of(MAT_ROWS * matrix, MAT_ROWS), MAT_ROWS)
        copy = pltpu.make_async_copy(source, moves.at[rows, :], sems.at[i])
        copy.start()
        loads.append(copy)
    for copy in loads:
        copy.wait()

    def rows_of(place):
        return pl.ds(pl.multiple_of(SHARD_ROWS * place, SHARD_ROWS), SHARD_ROWS)

    def store(place, i):
        rows = rows_of(place)
        return pltpu.make_async_copy(results.at[rows, :], weights.at[rows, :], stores.at[i])

    for i, (source, (partner, second, _)) in enumerate(zip(sources, QUADS)):

        def weigh(slot, carry):
            place = held(info, partner, second, slot)
            rows = rows_of(place)
            kept = source[rows_of(slot), :].astype(f32) * KEEP
            results[rows, :] = (kept - RATE * moves[rows, :].astype(f32)).astype(bf16)
            store(place, 4 * i + slot).start()
            return carry

        lax.fori_loop(0, 4, weigh, 0)

    for _, slot, place in arrivals(info, [None], QUADS[7:]):
        rest_ref[SHARD_ROWS * slot : SHARD_ROWS * slot + SHARD_ROWS, :] = moves[rows_of(place), :]
    update = math.sqrt(D) * moves[rows_of(shard), :].astype(f32)
    update_ref[...] = update
    new_ref[...] = master_ref[...] * KEEP - learn_rate * 0.2 * update
    for i, (_, slot, place) in enumerate(arrivals(info, sources, QUADS[:7])):
        store(place, i).wait()


def closing_kernel(info, _, rest, masters, weights, results, stores):
    written = []
    for i, (_, _, place) in enumerate(arrivals(info, [None], QUADS[7:])):
        part = slice(SHARD_ROWS * i, SHARD_ROWS * i + SHARD_ROWS)
        kept = masters[part, :].astype(f32) * KEEP
        results[part, :] = (kept - RATE * rest[part, :].astype(f32)).astype(bf16)
        rows = pl.ds(pl.multiple_of(SHARD_ROWS * place, SHARD_ROWS), SHARD_ROWS)
        copy = pltpu.make_async_copy(results.at[part, :], weights.at[rows, :], stores.at[i])
        copy.start()
        written.append(copy)
    for copy in written:
        copy.wait()


def params(mib):
    return pltpu.CompilerParams(vmem_limit_bytes=mib * MIB)


def joined(blocks, parts):
    lengths = [4 * blocks[0].shape[0]] + [2 * blocks[0].shape[0]] * (parts - 1)
    return pl.pallas_call(
        join_kernel,
        out_shape=tuple(jax.ShapeDtypeStruct((n,) + blocks[0].shape[1:], bf16) for n in lengths),
        in_specs=[VM] * 4,
        out_specs=(VM,) * parts,
        compiler_params=params(8),
    )(*blocks)


def on_device(gradient, momentum, master_weights, slot_table):
    group = lax.axis_index("group").astype(jnp.int32)
    shard = lax.axis_index("shard").astype(jnp.int32)
    info = jnp.concatenate([slot_table, jnp.stack([group, shard]), held_table(shard)])
    gradient = gradient.reshape(SHARD_ROWS, 128)
    momentum = momentum.reshape(SHARD_ROWS, 128)
    master_weights = master_weights.reshape(SHARD_ROWS, 128)

    def send(block, route):
        return lax.ppermute(block, "shard", route)

    sums, narrow = pl.pallas_call(
        opening_kernel,
        out_shape=(
            jax.ShapeDtypeStruct((32, 128), f32),
            jax.ShapeDtypeStruct((SHARD_ROWS, 128), bf16),
        ),
        in_specs=[HBM, HBM],
        out_specs=(VM, VM),
        scratch_shapes=[
            pltpu.VMEM((SHARD_ROWS, 128), f32),
            pltpu.VMEM((SHARD_ROWS, 128), f32),
            pltpu.SemaphoreType.DMA((4,)),
        ],
        compiler_params=params(60),
    )(gradient, master_weights)
    masters = [narrow] + [send(narrow, first_route(step)) for step in (1, 2, 3)]
    sums = lax.all_to_all(sums, "shard", 0, 0)
    sums = jnp.broadcast_to(jnp.sum(sums, axis=0, keepdims=True), (8, 128))
    (quad,) = joined(masters, 1)
    quad, sums = lax.optimization_barrier((quad, sums))
    sums = lax.all_to_all(sums, "group", 0, 0)

    flat_shape = jax.ShapeDtypeStruct((SHARD_ROWS, 128), f32)
    new_momentum, look = pl.pallas_call(
        look_kernel,
        out_shape=(flat_shape, jax.ShapeDtypeStruct((SHARD_TILES, 16, 128), bf16)),
        in_specs=[SM, VM, VM, VM],
        out_specs=(VM, VM),
        scratch_shapes=[pltpu.VMEM((SHARD_ROWS, 128), f32)],
        compiler_params=params(8),
    )(info, sums, gradient, momentum)

    whole, ahead, behind = joined([look] + [send(look, first_route(step)) for step in (1, 2, 3)], 3)
    forward = [send(ahead, second_route(1)), send(behind, second_route(1))]
    backward = [send(ahead, second_route(3)), send(behind, second_route(3))]
    across = [send(forward[0], second_route(1)), send(backward[1], second_route(3))]
    whole, forward[0] = lax.optimization_barrier((whole, forward[0]))
    early = [whole, forward[0], backward[1], forward[1], backward[0]]
    swapped = [send(block, swap_route()) for block in early]
    across, swapped = lax.optimization_barrier((across, swapped))
    quad, across = lax.optimization_barrier((quad, across))
    sources = early + across + swapped + [send(block, swap_route()) for block in across]
    masters = [quad, send(quad, second_route(1)), send(quad, second_route(3))]

    cost = pl.CostEstimate(flops=9_300_000_000, bytes_accessed=20_000_000, transcendentals=0)

    def orthogonalized(last):
        return pl.pallas_call(
            lambda *refs: matrix_kernel(last, *refs),
            out_shape=jax.ShapeDtypeStruct((MAT_ROWS, 128), bf16),
            in_specs=[SM] + [HBM] * 14,
            out_specs=VM,
            scratch_shapes=MATRIX_SCRATCH,
            compiler_params=params(29),
            cost_estimate=cost,
        )(info, *sources)

    mine = orthogonalized(False)
    mine, masters = lax.optimization_barrier((mine, masters))
    theirs = send(mine, swap_route())
    across = send(masters[1], second_route(1))
    masters = masters + [across] + [send(block, swap_route()) for block in masters]
    third = orthogonalized(True)
    third, across = lax.optimization_barrier((third, across))
    last = send(across, swap_route())
    weights_shape = jax.ShapeDtypeStruct((MATS * MAT_ROWS, 128), bf16)
    quad_shape = jax.ShapeDtypeStruct((4 * SHARD_ROWS, 128), bf16)
    weights, update, new_master, rest = pl.pallas_call(
        finish_kernel,
        out_shape=(weights_shape, flat_shape, flat_shape, quad_shape),
        in_specs=[SM] + [VM] * 11,
        out_specs=(ANY, VM, VM, VM),
        scratch_shapes=[
            pltpu.VMEM((MATS * MAT_ROWS, 128), bf16),
            pltpu.VMEM((MATS * MAT_ROWS, 128), bf16),
            pltpu.SemaphoreType.DMA((3,)),
            pltpu.SemaphoreType.DMA((28,)),
        ],
        compiler_params=params(24),
        cost_estimate=pl.CostEstimate(flops=10_000_000, bytes_accessed=28_000_000, transcendentals=0),
    )(info, mine, theirs, third, master_weights, *masters)
    weights = pl.pallas_call(
        closing_kernel,
        out_shape=weights_shape,
        in_specs=[SM, ANY, VM, VM],
        out_specs=ANY,
        scratch_shapes=[
            pltpu.VMEM((4 * SHARD_ROWS, 128), bf16),
            pltpu.SemaphoreType.DMA((4,)),
        ],
        input_output_aliases={1: 0},
        compiler_params=params(16),
    )(info, weights, rest, last)
    return (
        new_momentum.reshape(-1),
        update.reshape(-1),
        new_master.reshape(-1),
        weights.reshape(-1),
    )


def solution(mesh):
    in_specs = (P(("group", "shard")), P(("group", "shard")), P(("group", "shard")), P())
    out_specs = (P(("group", "shard")), P(("group", "shard")), P(("group", "shard")), P("group"))
    return jax.shard_map(
        on_device, mesh=mesh, in_specs=in_specs, out_specs=out_specs, check_vma=False
    )
```

```python
import math

import jax
import jax.numpy as jnp
from jax import lax
from jax.experimental import pallas as pl
from jax.experimental.pallas import tpu as pltpu
from jax.sharding import PartitionSpec as P

D = 2048
FF = 768
MATS = 3
UNITS = 32
SHARD_TILES = 72
SHARD_ROWS = 1152
MAT_ROWS = 12288
MAT_TILES = 768
WIDE = 256

coef_first = 3.4445
coef_second = -4.775
coef_third = 2.0315
beta_momentum = 0.95
learn_rate = 0.02
weight_decay = 0.1

f32 = jnp.float32
bf16 = jnp.bfloat16
MIB = 2**20

VM = pl.BlockSpec(memory_space=pltpu.VMEM)
SM = pl.BlockSpec(memory_space=pltpu.SMEM)
ANY = pl.BlockSpec(memory_space=pl.ANY)
HBM = pl.BlockSpec(memory_space=pltpu.HBM)


def shard_of(x, y, c):
    return (x % 4) * 8 + (y % 4) * 2 + c


def first_route(step):
    route = []
    for x in range(4):
        for y in range(4):
            route.append((shard_of(x, y, 0), shard_of(x, y + step, 0)))
            route.append((shard_of(x, y, 1), shard_of(x + step, y, 1)))
    return route


def second_route(step):
    route = []
    for x in range(4):
        for y in range(4):
            route.append((shard_of(x, y, 0), shard_of(x + step, y, 0)))
            route.append((shard_of(x, y, 1), shard_of(x, y + step, 1)))
    return route


def swap_route():
    return [(s, s ^ 1) for s in range(32)]


def kind_of(info, matrix):
    kind = jnp.int32(0)
    for m in range(24):
        kind = jnp.where(info[m] == matrix, jnp.int32(m % 3), kind)
    return kind


def opening_kernel(g_in, master_in, sums_ref, narrow_ref, g_ref, master_ref, sems):
    half = SHARD_ROWS // 2
    loads = []
    for i, (source, target) in enumerate(((g_in, g_ref), (master_in, master_ref))):
        for n in range(2):
            rows = pl.ds(half * n, half)
            copy = pltpu.make_async_copy(source.at[rows, :], target.at[rows, :], sems.at[2 * i + n])
            copy.start()
            loads.append(copy)
    total = jnp.zeros((8, 128), f32)
    for n in range(2):
        loads[n].wait()
        gradient = g_ref[half * n : half * n + half, :]
        total = total + jnp.sum((gradient * gradient).reshape(half // 8, 8, 128), axis=0)
    total = jnp.sum(jnp.sum(total, axis=0, keepdims=True), axis=1, keepdims=True)
    sums_ref[...] = jnp.broadcast_to(total, (32, 128))
    for n in range(2):
        loads[2 + n].wait()
        rows = slice(half * n, half * n + half)
        narrow_ref[rows, :] = master_ref[rows, :].astype(bf16)


def join_kernel(*refs):
    for out, taken in zip(refs[4:], (refs[:4], refs[:2], refs[2:4])):
        length = taken[0].shape[0]
        for i, ref in enumerate(taken):
            out[length * i : length * i + length] = ref[...]


def join_masters_kernel(own, near, far, back, out, sems):
    copy = pltpu.make_async_copy(own, out.at[pl.ds(0, SHARD_ROWS), :], sems.at[0])
    copy.start()
    for i, ref in enumerate((near, far, back)):
        out[SHARD_ROWS * (i + 1) : SHARD_ROWS * (i + 2), :] = ref[...]
    copy.wait()


def look_kernel(info, sums, g_ref, m_ref, nm_ref, look_ref, scratch):
    total = jnp.sum(sums[...], axis=0, keepdims=True)[:, :1]
    clip = jnp.minimum(1.0, 0.5 * math.sqrt(24 * D * FF) / jnp.sqrt(total + 1e-06))
    clipped = clip * g_ref[...]
    new_momentum = beta_momentum * m_ref[...] + clipped
    nm_ref[...] = new_momentum
    scratch[...] = clipped + beta_momentum * new_momentum
    group, shard = info[24], info[25]
    for t in range(3):
        kind = kind_of(info, 3 * group + (3 * shard + t) // UNITS)
        row = 384 * t

        @pl.when(kind != 2)
        def _():
            for a in range(4):
                for j in range(6):
                    tile = scratch[pl.ds(row + 96 * a + j, 16, stride=6), :]
                    look_ref[24 * t + 6 * a + j] = tile.astype(bf16)

        @pl.when(kind == 2)
        def _():
            for j in range(16):
                tile = scratch[pl.ds(row + j, 16, stride=16), :]
                look_ref[24 * t + j] = tile.astype(bf16)
            for q in range(8):
                low = scratch[pl.ds(row + 256 + q, 8, stride=16), :]
                high = scratch[pl.ds(row + 264 + q, 8, stride=16), :]
                look_ref[24 * t + 16 + q] = jnp.concatenate([low, high], 0).astype(bf16)


def tiles(x, first, count, stride):
    return jnp.concatenate([x[first + stride * i] for i in range(count)], 0)


def mm(a, b):
    return jnp.dot(a, b, preferred_element_type=f32)


def mm_t(a, b):
    return lax.dot_general(a, b, (((1,), (1,)), ((), ())), preferred_element_type=f32)


def orthogonalize(kind, base, x, wide, flat, a0, b0, wb, b1, total, emit):
    @pl.when(kind == 2)
    def _():
        def pair(i, carry):
            t = base + 48 * i
            for h in range(2):
                rows = pl.ds(pl.multiple_of(32 * i + 16 * h, 16), 16)
                for j in range(16):
                    wide[rows, 128 * j : 128 * j + 128] = x[t + 24 * h + j]
            rows = pl.ds(pl.multiple_of(512 + 16 * i, 16), 16)
            for q in range(8):
                one = x[t + 16 + q].astype(f32)
                two = x[t + 40 + q].astype(f32)
                low = jnp.concatenate([one[:8], two[:8]], 0).astype(bf16)
                high = jnp.concatenate([one[8:], two[8:]], 0).astype(bf16)
                wide[rows, 128 * q : 128 * q + 128] = low
                wide[rows, 128 * (q + 8) : 128 * (q + 8) + 128] = high
            return carry

        lax.fori_loop(0, 16, pair, 0)

    @pl.when(kind != 2)
    def _():
        def chunk(i, carry):
            columns = pl.ds(pl.multiple_of(WIDE * i, WIDE), WIDE)
            for j in range(6):
                wide[128 * j : 128 * j + 128, columns] = tiles(x, base + 96 * i + j, 16, 6).T
            return carry

        lax.fori_loop(0, 8, chunk, 0)

    parts = [slice(WIDE * n, WIDE * n + WIDE) for n in range(3)]
    lower = [slice(WIDE * n, FF) for n in range(3)]
    iota = lax.broadcasted_iota

    def mirror(target, n):
        for m in range(n + 1, 3):
            target[parts[n], parts[m]] = target[parts[m], parts[n]].T

    square_sum = jnp.zeros((1, 1), f32)
    same = iota(jnp.int32, (WIDE, WIDE), 0) == iota(jnp.int32, (WIDE, WIDE), 1)
    for n, part in enumerate(parts):
        total[lower[n], part] = mm_t(wide[lower[n], :], wide[part, :])
        square_sum = square_sum + jnp.sum(jnp.where(same, total[part, part], 0.0), keepdims=True)
    inverse = 1.0 / (jnp.sqrt(square_sum) + 1e-07)
    for n, part in enumerate(parts):
        a0[lower[n], part] = (total[lower[n], part] * inverse * inverse).astype(bf16)
        mirror(a0, n)
    for n, part in enumerate(parts):
        square = mm(a0[lower[n], :], a0[:, part])
        poly = coef_second * a0[lower[n], part].astype(f32) + coef_third * square
        b0[lower[n], part] = poly.astype(bf16)
        mirror(b0, n)
    for n, part in enumerate(parts):
        step = coef_first * a0[lower[n], part].astype(f32) + mm(a0[lower[n], :], b0[:, part])
        total[lower[n], part] = coef_first * step
        wb[lower[n], part] = step.astype(bf16)
        mirror(wb, n)
    a1 = a0
    for n, part in enumerate(parts):
        step = total[lower[n], part] + mm(b0[lower[n], :], wb[:, part])
        a1[lower[n], part] = step.astype(bf16)
        mirror(a1, n)
    for n, part in enumerate(parts):
        square = mm(a1[lower[n], :], a1[:, part])
        poly = coef_second * a1[lower[n], part].astype(f32) + coef_third * square
        b1[lower[n], part] = poly.astype(bf16)
        mirror(b1, n)
    scale = inverse
    rest = wb
    diagonal_row = []
    diagonal_column = []
    for n, part in enumerate(parts):
        both = b0[lower[n], part].astype(f32) + b1[lower[n], part].astype(f32)
        step = coef_first * both + mm(b1[lower[n], :], b0[:, part])
        top = jnp.where(same, step[:WIDE], 0.0)
        diagonal_row.append(jnp.sum(top, axis=0, keepdims=True))
        diagonal_column.append(jnp.sum(top, axis=1, keepdims=True))
        rest[part, part] = (jnp.where(same, 0.0, step[:WIDE]) * scale).astype(bf16)
        if n < 2:
            rest[lower[n + 1], part] = (step[WIDE:] * scale).astype(bf16)
        mirror(rest, n)
    diagonal_column = jnp.concatenate(diagonal_column, 0)
    diagonal_row = (jnp.concatenate(diagonal_row, 1) + coef_first * coef_first) * scale
    diagonal_column = (diagonal_column + coef_first * coef_first) * scale

    @pl.when(kind != 2)
    def _():
        def chunk(i, carry):
            block = jnp.concatenate([tiles(x, base + 192 * i + j, 32, 6) for j in range(6)], 1)
            moved = mm(block, rest[...]) + block.astype(f32) * diagonal_row
            for j in range(6):
                rows = pl.ds(3072 * i + j, 2 * WIDE, stride=6)
                flat[rows, :] = moved[:, 128 * j : 128 * j + 128]
            emit(2 * i)
            emit(2 * i + 1)
            return carry

        lax.fori_loop(0, 4, chunk, 0)

    @pl.when(kind == 2)
    def _():
        def chunk(i, carry):
            block = wide[:, pl.ds(pl.multiple_of(WIDE * i, WIDE), WIDE)]
            moved = mm(rest[...], block) + block.astype(f32) * diagonal_column
            for h in range(2):
                panel = moved[:, 128 * h : 128 * h + 128]
                start = 2 * i + h
                for u in range(UNITS):
                    rows = pl.ds(start + 384 * u, 16, stride=16)
                    flat[rows, :] = panel[16 * u : 16 * u + 16]
                    rows = pl.ds(start + 384 * u + 256, 8, stride=16)
                    flat[rows, :] = panel[512 + 8 * u : 512 + 8 * u + 8]
            return carry

        lax.fori_loop(0, 8, chunk, 0)

        def emit_one(i, carry):
            emit(i)
            return carry

        lax.fori_loop(0, 8, emit_one, 0)


def held_table(shard):
    n = jnp.arange(32, dtype=jnp.int32)
    partner, hops = n // 16, n % 4
    second = (n // 4) % 4
    second = jnp.where(second < 2, second, 5 - second)
    row, column, core = shard // 8, (shard // 2) % 4, shard % 2
    holder = core + partner - 2 * core * partner
    at_zero = shard_of(row - second + 4, column - hops + 4, 0)
    at_one = shard_of(row - hops + 4, column - second + 4, 1)
    return jnp.where(holder == 0, at_zero, at_one)


def held(info, partner, second, hops):
    return info[26 + 16 * int(partner) + 4 * HOPS.index(second) + hops]


def arrivals(info, sources, slots):
    found = []
    for source, (partner, second, first_hops) in zip(sources, slots):
        for slot, hops in enumerate(first_hops):
            found.append((source, slot, held(info, partner, second, hops)))
    return found


def matrix_kernel(last, *refs):
    info, sources, refs = refs[0], refs[1:15], refs[15:]
    result, x, wide, flat, a0, b0, wb, b1, total, sems = refs
    group, shard = info[24], info[25]
    matrix = jnp.int32(2) if last else shard % 2
    first = (UNITS * matrix) // 3
    final = (UNITS * matrix + UNITS - 1) // 3
    loads = []
    for i, (source, slot, place) in enumerate(arrivals(info, sources, BLOCKS)):
        wanted = (place >= first) & (place <= final)
        target = SHARD_TILES * jnp.clip(place - first, 0, 11)
        copy = pltpu.make_async_copy(
            source.at[pl.ds(SHARD_TILES * slot, SHARD_TILES)],
            x.at[pl.ds(target, SHARD_TILES)],
            sems.at[i],
        )
        loads.append((wanted, copy))
    for wanted, copy in loads:
        pl.when(wanted)(copy.start)
    for wanted, copy in loads:
        pl.when(wanted)(copy.wait)

    kind = kind_of(info, 3 * group + matrix)
    base = MAT_TILES * matrix - SHARD_TILES * first

    def emit(i):
        rows = pl.ds(pl.multiple_of(1536 * i, 1536), 1536)
        result[rows, :] = flat[rows, :].astype(bf16)

    orthogonalize(kind, base, x, wide, flat, a0, b0, wb, b1, total, emit)


HOPS = (0, 1, 3, 2)
BLOCKS = [
    (p, q, dp)
    for p in (False, True)
    for q, dp in ((0, (0, 1, 2, 3)), (1, (0, 1)), (3, (2, 3)), (1, (2, 3)), (3, (0, 1)))
]
BLOCKS = BLOCKS[:5] + [(False, 2, (0, 1)), (False, 2, (2, 3))] + BLOCKS[5:]
BLOCKS = BLOCKS + [(True, 2, (0, 1)), (True, 2, (2, 3))]
QUADS = [(p, q, (0, 1, 2, 3)) for p in (False, True) for q in HOPS]


MATRIX_SCRATCH = [
    pltpu.VMEM((12 * SHARD_TILES, 16, 128), bf16),
    pltpu.VMEM((FF, D), bf16),
    pltpu.VMEM((MAT_ROWS, 128), f32),
    pltpu.VMEM((FF, FF), bf16),
    pltpu.VMEM((FF, FF), bf16),
    pltpu.VMEM((FF, FF), bf16),
    pltpu.VMEM((FF, FF), bf16),
    pltpu.VMEM((FF, FF), f32),
    pltpu.SemaphoreType.DMA((32,)),
]


KEEP = 1.0 - learn_rate * weight_decay
RATE = learn_rate * 0.2 * math.sqrt(D)


def finish_kernel(info, *refs):
    mine, theirs, third, master_ref = refs[:4]
    sources = refs[4:11]
    weights, update_ref, new_ref, rest_ref, moves, results, sems, stores = refs[11:]
    shard = info[25]
    core = shard % 2
    loads = []
    for i, (source, matrix) in enumerate(((mine, core), (theirs, 1 - core), (third, 2))):
        rows = pl.ds(pl.multiple_of(MAT_ROWS * matrix, MAT_ROWS), MAT_ROWS)
        copy = pltpu.make_async_copy(source, moves.at[rows, :], sems.at[i])
        copy.start()
        loads.append(copy)
    for copy in loads:
        copy.wait()

    def rows_of(place):
        return pl.ds(pl.multiple_of(SHARD_ROWS * place, SHARD_ROWS), SHARD_ROWS)

    def store(place, i):
        rows = rows_of(place)
        return pltpu.make_async_copy(results.at[rows, :], weights.at[rows, :], stores.at[i])

    for i, (source, (partner, second, _)) in enumerate(zip(sources, QUADS)):

        def weigh(slot, carry):
            place = held(info, partner, second, slot)
            rows = rows_of(place)
            kept = source[rows_of(slot), :].astype(f32) * KEEP
            results[rows, :] = (kept - RATE * moves[rows, :].astype(f32)).astype(bf16)
            store(place, 4 * i + slot).start()
            return carry

        lax.fori_loop(0, 4, weigh, 0)

    for _, slot, place in arrivals(info, [None], QUADS[7:]):
        rest_ref[SHARD_ROWS * slot : SHARD_ROWS * slot + SHARD_ROWS, :] = moves[rows_of(place), :]
    update = math.sqrt(D) * moves[rows_of(shard), :].astype(f32)
    update_ref[...] = update
    new_ref[...] = master_ref[...] * KEEP - learn_rate * 0.2 * update
    for i, (_, slot, place) in enumerate(arrivals(info, sources, QUADS[:7])):
        store(place, i).wait()


def closing_kernel(info, _, rest, masters, weights, results, stores):
    written = []
    for i, (_, _, place) in enumerate(arrivals(info, [None], QUADS[7:])):
        part = slice(SHARD_ROWS * i, SHARD_ROWS * i + SHARD_ROWS)
        kept = masters[part, :].astype(f32) * KEEP
        results[part, :] = (kept - RATE * rest[part, :].astype(f32)).astype(bf16)
        rows = pl.ds(pl.multiple_of(SHARD_ROWS * place, SHARD_ROWS), SHARD_ROWS)
        copy = pltpu.make_async_copy(results.at[part, :], weights.at[rows, :], stores.at[i])
        copy.start()
        written.append(copy)
    for copy in written:
        copy.wait()


def params(mib):
    return pltpu.CompilerParams(vmem_limit_bytes=mib * MIB)


def joined(blocks, parts):
    lengths = [4 * blocks[0].shape[0]] + [2 * blocks[0].shape[0]] * (parts - 1)
    return pl.pallas_call(
        join_kernel,
        out_shape=tuple(jax.ShapeDtypeStruct((n,) + blocks[0].shape[1:], bf16) for n in lengths),
        in_specs=[VM] * 4,
        out_specs=(VM,) * parts,
        compiler_params=params(8),
    )(*blocks)


def on_device(gradient, momentum, master_weights, slot_table):
    group = lax.axis_index("group").astype(jnp.int32)
    shard = lax.axis_index("shard").astype(jnp.int32)
    info = jnp.concatenate([slot_table, jnp.stack([group, shard]), held_table(shard)])
    gradient = gradient.reshape(SHARD_ROWS, 128)
    momentum = momentum.reshape(SHARD_ROWS, 128)
    master_weights = master_weights.reshape(SHARD_ROWS, 128)

    def send(block, route):
        return lax.ppermute(block, "shard", route)

    sums, narrow = pl.pallas_call(
        opening_kernel,
        out_shape=(
            jax.ShapeDtypeStruct((32, 128), f32),
            jax.ShapeDtypeStruct((SHARD_ROWS, 128), bf16),
        ),
        in_specs=[HBM, HBM],
        out_specs=(VM, VM),
        scratch_shapes=[
            pltpu.VMEM((SHARD_ROWS, 128), f32),
            pltpu.VMEM((SHARD_ROWS, 128), f32),
            pltpu.SemaphoreType.DMA((4,)),
        ],
        compiler_params=params(60),
    )(gradient, master_weights)
    masters = [narrow] + [send(narrow, first_route(step)) for step in (1, 2, 3)]
    sums = lax.all_to_all(sums, "shard", 0, 0)
    sums = jnp.broadcast_to(jnp.sum(sums, axis=0, keepdims=True), (8, 128))
    quad = pl.pallas_call(
        join_masters_kernel,
        out_shape=jax.ShapeDtypeStruct((4 * SHARD_ROWS, 128), bf16),
        in_specs=[HBM, VM, VM, VM],
        out_specs=VM,
        scratch_shapes=[pltpu.SemaphoreType.DMA((1,))],
        compiler_params=params(56),
    )(*masters)
    quad, sums = lax.optimization_barrier((quad, sums))
    sums = lax.all_to_all(sums, "group", 0, 0)

    flat_shape = jax.ShapeDtypeStruct((SHARD_ROWS, 128), f32)
    new_momentum, look = pl.pallas_call(
        look_kernel,
        out_shape=(flat_shape, jax.ShapeDtypeStruct((SHARD_TILES, 16, 128), bf16)),
        in_specs=[SM, VM, VM, VM],
        out_specs=(VM, VM),
        scratch_shapes=[pltpu.VMEM((SHARD_ROWS, 128), f32)],
        compiler_params=params(8),
    )(info, sums, gradient, momentum)

    whole, ahead, behind = joined([look] + [send(look, first_route(step)) for step in (1, 2, 3)], 3)
    forward = [send(ahead, second_route(1)), send(behind, second_route(1))]
    backward = [send(ahead, second_route(3)), send(behind, second_route(3))]
    across = [send(forward[0], second_route(1)), send(backward[1], second_route(3))]
    whole, forward[0] = lax.optimization_barrier((whole, forward[0]))
    early = [whole, forward[0], backward[1], forward[1], backward[0]]
    swapped = [send(block, swap_route()) for block in early]
    across, swapped = lax.optimization_barrier((across, swapped))
    quad, across = lax.optimization_barrier((quad, across))
    sources = early + across + swapped + [send(block, swap_route()) for block in across]
    masters = [quad, send(quad, second_route(1)), send(quad, second_route(3))]

    cost = pl.CostEstimate(flops=9_300_000_000, bytes_accessed=20_000_000, transcendentals=0)

    def orthogonalized(last):
        return pl.pallas_call(
            lambda *refs: matrix_kernel(last, *refs),
            out_shape=jax.ShapeDtypeStruct((MAT_ROWS, 128), bf16),
            in_specs=[SM] + [HBM] * 14,
            out_specs=VM,
            scratch_shapes=MATRIX_SCRATCH,
            compiler_params=params(29),
            cost_estimate=cost,
        )(info, *sources)

    mine = orthogonalized(False)
    mine, masters = lax.optimization_barrier((mine, masters))
    theirs = send(mine, swap_route())
    across = send(masters[1], second_route(1))
    masters = masters + [across] + [send(block, swap_route()) for block in masters]
    third = orthogonalized(True)
    third, across = lax.optimization_barrier((third, across))
    last = send(across, swap_route())
    weights_shape = jax.ShapeDtypeStruct((MATS * MAT_ROWS, 128), bf16)
    quad_shape = jax.ShapeDtypeStruct((4 * SHARD_ROWS, 128), bf16)
    weights, update, new_master, rest = pl.pallas_call(
        finish_kernel,
        out_shape=(weights_shape, flat_shape, flat_shape, quad_shape),
        in_specs=[SM] + [VM] * 11,
        out_specs=(ANY, VM, VM, VM),
        scratch_shapes=[
            pltpu.VMEM((MATS * MAT_ROWS, 128), bf16),
            pltpu.VMEM((MATS * MAT_ROWS, 128), bf16),
            pltpu.SemaphoreType.DMA((3,)),
            pltpu.SemaphoreType.DMA((28,)),
        ],
        compiler_params=params(24),
        cost_estimate=pl.CostEstimate(flops=10_000_000, bytes_accessed=28_000_000, transcendentals=0),
    )(info, mine, theirs, third, master_weights, *masters)
    weights = pl.pallas_call(
        closing_kernel,
        out_shape=weights_shape,
        in_specs=[SM, ANY, VM, VM],
        out_specs=ANY,
        scratch_shapes=[
            pltpu.VMEM((4 * SHARD_ROWS, 128), bf16),
            pltpu.SemaphoreType.DMA((4,)),
        ],
        input_output_aliases={1: 0},
        compiler_params=params(16),
    )(info, weights, rest, last)
    return (
        new_momentum.reshape(-1),
        update.reshape(-1),
        new_master.reshape(-1),
        weights.reshape(-1),
    )


def solution(mesh):
    in_specs = (P(("group", "shard")), P(("group", "shard")), P(("group", "shard")), P())
    out_specs = (P(("group", "shard")), P(("group", "shard")), P(("group", "shard")), P("group"))
    return jax.shard_map(
        on_device, mesh=mesh, in_specs=in_specs, out_specs=out_specs, check_vma=False
    )
```
